32 devices in a mesh: seq: 4 (over x, core), utt: 8 (over z, y).
Axes of the slice: x: 2, y: 2, z: 4, core: 2. Of those that a mesh axis runs over, the one named last changes fastest.
Arguments:
- frames: bfloat16 [16, 1536, 768], P('utt', 'seq'), may hold values from -6 to 6
- lengths: int32 [16], P('utt'), may hold values from 512 to 1536, as said below
- drop_bits: int32 [16, 2], P('utt'), may hold values 0 or 1
- w_qkv: bfloat16 [2, 768, 2304], replicated, may hold values from -0.21875 to 0.21875
- attn_bias: float32 [2, 2, 768], replicated, may hold values from -0.03125 to 0.03125
- w_out: bfloat16 [2, 768, 768], replicated, may hold values from -4 to 4
- layer_bias: float32 [2, 4, 768], replicated, may hold values from -0.625 to 0.625
- gains: float32 [2, 2, 768], replicated, may hold values from 0.5 to 1.5
- w_in: bfloat16 [2, 768, 3072], replicated, may hold values from -0.21875 to 0.21875
- in_bias: float32 [2, 3072], replicated, may hold values from -0.625 to 0.625
- w_back: bfloat16 [2, 3072, 768], replicated, may hold values from -0.109375 to 0.109375
- cotangent: bfloat16 [16, 1536, 768], P('utt', 'seq'), may hold values from -6 to 6
Outputs:
- mixed: bfloat16 [16, 1536, 768], P('utt', 'seq')
- grad_frames: bfloat16 [16, 1536, 768], P('utt', 'seq')
- grad_qkv: float32 [2, 768, 2304], P(None, 'utt')
- grad_attn_bias: float32 [2, 2, 768], P(None, None, 'utt')
- grad_out_w: float32 [2, 768, 768], P(None, 'utt')
- grad_layer_bias: float32 [2, 4, 768], P(None, None, 'utt')
- grad_gains: float32 [2, 2, 768], P(None, None, 'utt')
- grad_in_w: float32 [2, 768, 3072], P(None, 'utt')
- grad_in_bias: float32 [2, 3072], P(None, 'utt')
- grad_back_w: float32 [2, 3072, 768], P(None, 'utt')
The draws below stay inside these ranges and needn't reach their ends.
Inputs may be any that keep to these rules, and one draw needn't show every extreme that they name: `lengths`: in each aligned block of 2 utterances (those of one index of utt) at least one utterance, which one drawn from the seed, has length 1536.
All inputs are finite; a program needn't handle non-finite values. No bound on the sum of `drop_bits` on one device may be relied on, other than what follows from the above.
Results may differ from the reference program's by a relative error of at most 0.02.
Values may be sent and summed in bfloat16 or wider, within the bound.
No kernel may reach another device: no remote copies, remote signals or barrier semaphores. Data moves between devices by JAX's collectives and lax.ppermute only.
A program may use at most 384 MiB of HBM per device.

```python
import jax
import jax.numpy as jnp
from jax import lax

D = 768
HEADS = 12
HEAD_DIM = 64
FF = 3072
LAYERS = 2
LENGTH = 1536
UTT_DEV = 2
UTTS = 16


def draw_lengths(key, part):
    key = jax.random.fold_in(key, 11)
    key_one, key_two = jax.random.split(key)
    random_len = jax.random.randint(key_one, (UTTS,), LENGTH // 3, LENGTH + 1)
    chosen = jax.random.randint(key_two, (UTTS // UTT_DEV,), 0, UTT_DEV)
    places = jnp.arange(UTTS, dtype=jnp.int32) % UTT_DEV
    filled = places == jnp.repeat(chosen, UTT_DEV)
    return jnp.where(filled, LENGTH, random_len).astype(jnp.int32)


def plant(drawn, own_key, low, largest):
    spot = [jax.random.randint(jax.random.fold_in(own_key, axis), (), 0, length) for axis, length in enumerate(drawn.shape)]
    widest = drawn.shape.index(max(drawn.shape))
    beside = spot[:widest] + [(spot[widest] + 1) % drawn.shape[widest]] + spot[widest + 1:]
    return drawn.at[tuple(spot)].set(low).at[tuple(beside)].set(largest)


def block_scale(rng, dims, pieces, smallest, high):
    def one(position, parts):
        heights = jax.random.uniform(jax.random.fold_in(jax.random.fold_in(rng, 6), position), (parts,), jnp.float32, smallest / len(pieces), high / len(pieces))
        return jnp.repeat(jnp.exp(heights), dims[position] // parts).reshape((-1,) + (1,) * (len(dims) - position - 1))

    gain = one(*pieces[0])
    for cut in pieces[1:]:
        gain = gain * one(*cut)
    return gain


def bell_draw(own_key, extent, deviation, most, cuts=(), kind=jnp.bfloat16):
    array = deviation * jax.random.normal(own_key, extent, jnp.float32)
    if cuts:
        array = array * block_scale(own_key, extent, cuts, -0.22, 0.18)
    return jnp.clip(array, -most, most).astype(kind)


def setup_inputs(seed: int = 0) -> dict:
    arg_keys = jax.random.split(jax.random.key(seed), 13)
    return {
        "frames": bell_draw(arg_keys[0], (UTTS, LENGTH, D), 1.0, 6.0, ((0, 8), (1, 4))),
        "lengths": draw_lengths(jax.random.fold_in(arg_keys[12], 71), 0),
        "drop_bits": plant((jax.random.randint(arg_keys[2], (UTTS, LAYERS), 0, 4) < 3).astype(jnp.int32), jax.random.fold_in(arg_keys[2], 1), 0, 1),
        "w_qkv": bell_draw(arg_keys[3], (LAYERS, D, 3 * D), D ** -0.5, 0.21875),
        "attn_bias": bell_draw(arg_keys[4], (LAYERS, 2, D), 0.005, 0.03125, (), jnp.float32),
        "w_out": bell_draw(arg_keys[5], (LAYERS, D, D), (max(1, D // (LENGTH // 4))) ** -0.5, 4.0),
        "layer_bias": bell_draw(arg_keys[6], (LAYERS, 4, D), 0.1, 0.625, (), jnp.float32),
        "gains": jnp.clip(1.0 + 0.1 * jax.random.normal(arg_keys[7], (LAYERS, 2, D), jnp.float32), 0.5, 1.5),
        "w_in": bell_draw(arg_keys[8], (LAYERS, D, FF), D ** -0.5, 0.21875),
        "in_bias": bell_draw(arg_keys[9], (LAYERS, FF), 0.1, 0.625, (), jnp.float32),
        "w_back": bell_draw(arg_keys[10], (LAYERS, FF, D), FF ** -0.5, 0.109375),
        "cotangent": bell_draw(arg_keys[11], (UTTS, LENGTH, D), 1.0, 6.0, ((0, 8), (1, 4))),
    }


@jax.custom_vjp
def low(v):
    return lax.optimization_barrier(v.astype(jnp.bfloat16)).astype(jnp.float32)

@jax.custom_vjp
def low_back(v):
    return v

def low_keep(v):
    return (low(v), None)

def low_pass(kept, grad):
    return (grad,)

def back_keep(v):
    return (v, None)

def back_low(kept, grad):
    return (low(grad),)
low.defvjp(low_keep, low_pass)
low_back.defvjp(back_keep, back_low)
masked_score = -1e+30

def matmul(left_side, right_side):
    return jnp.dot(left_side, right_side, precision=lax.Precision.HIGHEST)

def normalize(hidden, gain_vec, shift_vec):
    center = lax.optimization_barrier(jnp.mean(hidden, -1, keepdims=True))
    centred = hidden - center
    variance = lax.optimization_barrier(jnp.mean(centred * centred, -1, keepdims=True))
    return centred * lax.rsqrt(variance + 1e-05) * gain_vec + shift_vec

def gelu_exact(pre_act):
    return jax.nn.gelu(pre_act, approximate=False)

def encoder_layer(hidden, params, layer_index, length, live_bit):
    w_qkv, attn_bias, w_out, layer_bias, gains, w_in, in_bias, w_back = params
    seq_len, model_width = hidden.shape
    head_shape = (seq_len, HEADS, HEAD_DIM)
    lowered = low(hidden)
    projected = low_back(matmul(lowered, w_qkv[layer_index]))
    queries = low((projected[:, :model_width] + attn_bias[layer_index, 0]) * HEAD_DIM ** (-0.5))
    key_rows = low(projected[:, model_width:2 * model_width])
    value_rows = low(projected[:, 2 * model_width:] + attn_bias[layer_index, 1])
    scores = low_back(jnp.einsum('ihd,jhd->hij', queries.reshape(head_shape), key_rows.reshape(head_shape), precision=lax.Precision.HIGHEST))
    usable = jnp.arange(seq_len, dtype=jnp.int32) < length
    scores = jnp.where(usable[None, None, :], scores, masked_score)
    maximum = lax.optimization_barrier(jnp.max(scores, -1, keepdims=True))
    log_total = maximum + jnp.log(lax.optimization_barrier(jnp.sum(jnp.exp(scores - maximum), -1, keepdims=True)))
    attn_probs = low(jnp.exp(scores - log_total))
    attended = jnp.einsum('hij,jhd->ihd', attn_probs, value_rows.reshape(head_shape), precision=lax.Precision.HIGHEST).reshape(seq_len, model_width)
    attended = low(low_back(attended))
    first_sum = hidden + low_back(matmul(attended, w_out[layer_index])) + layer_bias[layer_index, 0]
    first_norm = normalize(first_sum, gains[layer_index, 0], layer_bias[layer_index, 1])
    pre_act = low_back(matmul(low(first_norm), w_in[layer_index])) + in_bias[layer_index]
    activated = low(gelu_exact(pre_act))
    second_sum = first_norm + low_back(matmul(activated, w_back[layer_index])) + layer_bias[layer_index, 2]
    second_norm = normalize(second_sum, gains[layer_index, 1], layer_bias[layer_index, 3])
    return jnp.where(live_bit > 0, second_norm, hidden)

def forward(frames_one, params, length, live_bits):
    hidden = frames_one
    for layer_index in range(LAYERS):
        hidden = encoder_layer(hidden, params, layer_index, length, live_bits[layer_index])
    return hidden

def reference(frames, lengths, drop_bits, w_qkv, attn_bias, w_out, layer_bias, gains, w_in, in_bias, w_back, cotangent):
    params = (w_qkv.astype(jnp.float32), attn_bias, w_out.astype(jnp.float32), layer_bias, gains, w_in.astype(jnp.float32), in_bias, w_back.astype(jnp.float32))

    def one_utterance(totals, element):
        utterance, length, live_bits, incoming = element

        def apply_all(frames_one, *weights):
            return forward(frames_one, weights, length, live_bits)
        outcome, pullback = jax.vjp(apply_all, utterance.astype(jnp.float32), *params)
        gradients = pullback(incoming.astype(jnp.float32))
        totals = tuple((running + update for running, update in zip(totals, gradients[1:])))
        return (totals, (outcome.astype(jnp.bfloat16), gradients[0].astype(jnp.bfloat16)))
    initial = tuple((jnp.zeros_like(member) for member in params))
    totals, (mixed_out, grad_frames) = lax.scan(one_utterance, initial, (frames, lengths, drop_bits, cotangent))
    return (mixed_out, grad_frames, totals[0], totals[1], totals[2], totals[3], totals[4], totals[5], totals[6], totals[7])
```

```python
import functools

import jax
import jax.numpy as jnp
from jax import lax
from jax.experimental import pallas as pl
from jax.experimental.pallas import tpu as pltpu
from jax.sharding import PartitionSpec as P

HEADS = 12
HEAD_DIM = 64
LAYERS = 2
LOG2E = 1.4426950408889634
LN2 = 0.6931471805599453
MASKED = -1e30
LANES = 128
MIB = 1 << 20

bf16 = jnp.bfloat16
f32 = jnp.float32


def dot(left, right):
    return jnp.dot(left, right, preferred_element_type=f32)


def dot_nt(left, right):
    return lax.dot_general(left, right, (((1,), (1,)), ((), ())), preferred_element_type=f32)


def dot_tn(left, right):
    return lax.dot_general(left, right, (((0,), (0,)), ((), ())), preferred_element_type=f32)


def row_step(rows):
    for step in (256, 192, 128, 96, 64, 32, 16):
        if rows % step == 0:
            return step
    return rows


def project_kernel(x_ref, w_ref, bias_ref, scale_ref, out_ref):
    low = x_ref[...].astype(bf16)
    out_ref[...] = ((dot(low, w_ref[0]) + bias_ref[...]) * scale_ref[...]).astype(bf16)


def project(x, w_qkv, layer, bias, scale, first, width, block=256):
    rows, model = x.shape
    return pl.pallas_call(
        project_kernel,
        grid=(width // block,),
        in_specs=[
            pl.BlockSpec((rows, model), lambda i: (0, 0)),
            pl.BlockSpec((1, model, block), lambda i: (layer, 0, i + first // block)),
            pl.BlockSpec((1, block), lambda i: (0, i + first // block)),
            pl.BlockSpec((1, block), lambda i: (0, i + first // block)),
        ],
        out_specs=pl.BlockSpec((rows, block), lambda i: (0, i)),
        out_shape=jax.ShapeDtypeStruct((rows, width), bf16),
        compiler_params=pltpu.CompilerParams(vmem_limit_bytes=40 * MIB),
        name="project",
    )(x, w_qkv, bias, scale)


def lane_index():
    return lax.broadcasted_iota(jnp.int32, (1, LANES), 1)


def head_lanes(head):
    lane = lane_index()
    own = (lane < HEAD_DIM) if head == 0 else (lane >= HEAD_DIM)
    return jnp.where(own, 1.0, 0.0).astype(bf16), jnp.where(own, 0.0, 1.0).astype(bf16)


def fill_key_columns(length_ref, base_ref, columns_ref, block_rows):
    @pl.when(pl.program_id(0) == 0)
    def _():
        for block in range(columns_ref.shape[0] // block_rows):
            row = lax.broadcasted_iota(jnp.int32, (block_rows, LANES), 0) + base_ref[block]
            slot = lax.broadcasted_iota(jnp.int32, (block_rows, LANES), 1) & (HEAD_DIM - 1)
            mask = jnp.where(row < length_ref[0], 0.0, MASKED)
            column = jnp.where(slot == 3, mask, jnp.where(slot < 3, 1.0, 0.0))
            columns_ref[block * block_rows : (block + 1) * block_rows] = column.astype(bf16)


def split_parts(value, last):
    slot = lane_index() & (HEAD_DIM - 1)
    high = value.astype(bf16).astype(f32)
    rest = value - high
    middle = rest.astype(bf16).astype(f32)
    low = rest - middle
    tail = jnp.where(slot == 2, low, jnp.where(slot == 3, last, 0.0))
    return jnp.where(slot == 0, high, jnp.where(slot == 1, middle, tail)).astype(bf16)


def attend_kernel(length_ref, base_ref, q_ref, *refs, parts, block_rows, step):
    key_refs = refs[:parts]
    value_refs = refs[parts : 2 * parts]
    out_ref, extra_ref, columns_ref = refs[2 * parts :]
    rows = q_ref.shape[0]
    fill_key_columns(length_ref, base_ref, columns_ref, block_rows)
    lane = lane_index()
    slot = lane & (HEAD_DIM - 1)

    def operands(head):
        own, other = head_lanes(head)
        constant = jnp.where(slot == 3, 1.0, 0.0).astype(bf16) * other
        keys, values = [], []
        offset = 0
        for key_ref, value_ref in zip(key_refs, value_refs):
            size = key_ref.shape[0]
            keys.append(key_ref[...] * own + columns_ref[offset : offset + size] * other)
            values.append(value_ref[...] * own + other)
            offset += size
        return own, constant, keys, values

    def finish(start, size, sums, shifts):
        top = jnp.where(lane < HEAD_DIM, sums[0], sums[1])
        total = jnp.where(lane < HEAD_DIM, sums[1], sums[0])
        out_ref[pl.ds(start, size)] = (top / pltpu.roll(total, HEAD_DIM, 1)).astype(bf16)
        log_total = jnp.log2(total)
        if shifts is not None:
            log_total = log_total + jnp.where(lane < HEAD_DIM, shifts[1], shifts[0])
        extra_ref[pl.ds(start, size)] = split_parts(-log_total, 1.0)
        return total

    all_sums = []
    for head in range(2):
        own, constant, keys, values = operands(head)
        sums = []
        for start in range(0, rows, step):
            query = q_ref[start : start + step] * own + constant
            total = None
            for key, value in zip(keys, values):
                probs = jnp.exp2(dot_nt(query, key)).astype(bf16)
                term = dot(probs, value)
                total = term if total is None else total + term
            sums.append(total)
        all_sums.append(sums)
    bad = jnp.float32(0.0)
    for index, start in enumerate(range(0, rows, step)):
        total = finish(start, step, (all_sums[0][index], all_sums[1][index]), None)
        inside = (total > 2.0**-80) & (total < 2.0**100)
        bad = bad + jnp.sum(jnp.where(inside, 0.0, 1.0))

    @pl.when(bad > 0.0)
    def _():
        size = 16

        def body(index, carry):
            start = pl.multiple_of(index * size, size)
            sums, shifts = [], []
            for head in range(2):
                own, constant, keys, values = operands(head)
                query = q_ref[pl.ds(start, size)] * own + constant
                scores = [dot_nt(query, key) for key in keys]
                largest = functools.reduce(
                    jnp.maximum, [jnp.max(part, -1, keepdims=True) for part in scores]
                )
                total = None
                for part, value in zip(scores, values):
                    term = dot(jnp.exp2(part - largest).astype(bf16), value)
                    total = term if total is None else total + term
                sums.append(total)
                shifts.append(largest)
            finish(start, size, sums, shifts)
            return carry

        lax.fori_loop(0, rows // size, body, 0)


def attend(length, base, q, key_values, block_rows):
    rows, model = q.shape
    pairs = model // LANES
    parts = len(key_values)
    total = sum(part.shape[0] for part in key_values)
    scalar = pl.BlockSpec(memory_space=pltpu.SMEM)

    def column(size, shift=0):
        return pl.BlockSpec((size, LANES), lambda i: (0, i + shift))

    kernel = functools.partial(
        attend_kernel, parts=parts, block_rows=block_rows, step=row_step(rows)
    )
    return pl.pallas_call(
        kernel,
        grid=(pairs,),
        in_specs=[scalar, scalar, column(rows)]
        + [column(part.shape[0]) for part in key_values]
        + [column(part.shape[0], pairs) for part in key_values],
        out_specs=[column(rows), column(rows)],
        out_shape=[jax.ShapeDtypeStruct((rows, model), bf16)] * 2,
        scratch_shapes=[pltpu.VMEM((total, LANES), bf16)],
        compiler_params=pltpu.CompilerParams(vmem_limit_bytes=56 * MIB),
        name="attend",
    )(length, base, q, *key_values, *key_values)


def attend_back_kernel(length_ref, base_ref, q_ref, grad_ref, out_ref, extra_ref, *refs, parts, block_rows, step):
    key_refs = refs[:parts]
    value_refs = refs[parts : 2 * parts]
    grad_query_ref = refs[2 * parts]
    grad_key_refs = refs[2 * parts + 1 : 3 * parts + 1]
    grad_value_refs = refs[3 * parts + 1 : 4 * parts + 1]
    columns_ref = refs[4 * parts + 1]
    rows = q_ref.shape[0]
    fill_key_columns(length_ref, base_ref, columns_ref, block_rows)
    lane = lane_index()
    slot = lane & (HEAD_DIM - 1)
    value_column = jnp.where(slot < 3, 1.0, 0.0).astype(bf16)
    from_lane = lax.broadcasted_iota(jnp.int32, (LANES, LANES), 0)
    to_lane = lax.broadcasted_iota(jnp.int32, (LANES, LANES), 1)
    swap = jnp.where((from_lane < HEAD_DIM) != (to_lane < HEAD_DIM), -1.0, 0.0).astype(bf16)
    grad_keys = [None] * parts
    grad_values = [None] * parts
    heads = [head_lanes(head) for head in range(2)]
    offsets = []
    offset = 0
    for part in range(parts):
        offsets.append(offset)
        offset += key_refs[part].shape[0]

    def add(old, new):
        return new if old is None else old + new

    for start in range(0, rows, step):
        query, grad = q_ref[start : start + step], grad_ref[start : start + step]
        extra = extra_ref[start : start + step]
        product = grad.astype(f32) * out_ref[start : start + step].astype(f32)
        high = product.astype(bf16)
        low = (product - high.astype(f32)).astype(bf16)
        inner = split_parts(dot(high, swap) + dot(low, swap), 0.0)
        grad_query = None
        for head in range(2):
            own, other = heads[head]
            query_own, grad_own = query * own, grad * own
            query_full, grad_full = query_own + extra * other, grad_own + inner * other
            query_turned, grad_turned = query_own.T, grad_own.T
            for part in range(parts):
                size = key_refs[part].shape[0]
                key_own = key_refs[part][...] * own
                key_full = key_own + columns_ref[offsets[part] : offsets[part] + size] * other
                value_full = value_refs[part][...] * own + value_column * other
                probs = jnp.exp2(dot_nt(query_full, key_full))
                grad_scores = (probs * dot_nt(grad_full, value_full)).astype(bf16)
                grad_values[part] = add(grad_values[part], dot(grad_turned, probs.astype(bf16)))
                grad_keys[part] = add(grad_keys[part], dot(query_turned, grad_scores))
                grad_query = add(grad_query, dot(grad_scores, key_own))
        grad_query_ref[start : start + step] = (grad_query * HEAD_DIM**-0.5).astype(bf16)
    for part in range(parts):
        grad_key_refs[part][...] = (grad_keys[part] * LN2).T.astype(bf16)
        grad_value_refs[part][...] = grad_values[part].T.astype(bf16)


def attend_back(length, base, q, grad, out, extra, key_values, block_rows):
    rows, model = q.shape
    pairs = model // LANES
    parts = len(key_values)
    total = sum(part.shape[0] for part in key_values)
    scalar = pl.BlockSpec(memory_space=pltpu.SMEM)

    def column(size, shift=0):
        return pl.BlockSpec((size, LANES), lambda i: (0, i + shift))

    sizes = [part.shape[0] for part in key_values]
    kernel = functools.partial(
        attend_back_kernel, parts=parts, block_rows=block_rows, step=row_step(rows)
    )
    return pl.pallas_call(
        kernel,
        grid=(pairs,),
        in_specs=[scalar, scalar] + [column(rows)] * 4
        + [column(size) for size in sizes]
        + [column(size, pairs) for size in sizes],
        out_specs=[column(rows)] + [column(size) for size in sizes] * 2,
        out_shape=[jax.ShapeDtypeStruct((rows, model), bf16)]
        + [jax.ShapeDtypeStruct((size, model), bf16) for size in sizes] * 2,
        scratch_shapes=[pltpu.VMEM((total, LANES), bf16)],
        compiler_params=pltpu.CompilerParams(vmem_limit_bytes=60 * MIB),
        name="attend_back",
    )(length, base, q, grad, out, extra, *key_values, *key_values)


def norm_parts(value):
    mean = jnp.mean(value, -1, keepdims=True)
    centred = value - mean
    inverse = lax.rsqrt(jnp.mean(centred * centred, -1, keepdims=True) + 1e-05)
    return centred * inverse, inverse


def gelu_parts(pre):
    size = jnp.abs(pre)
    ratio = 1.0 / (1.0 + size * (0.3275911 * 0.7071067811865476))
    poly = 1.061405429 * ratio - 1.453152027
    poly = poly * ratio + 1.421413741
    poly = poly * ratio - 0.284496736
    poly = (poly * ratio + 0.254829592) * ratio
    bell = jnp.exp2(pre * pre * (-0.5 * LOG2E))
    tail = 0.5 * poly * bell
    share = jnp.where(pre < 0.0, tail, 1.0 - tail)
    return pre * share, share + pre * bell * 0.3989422804014327


def feed_kernel(
    live_ref, x_ref, att_ref, wout_ref, lbias_ref, gains_ref, win_ref, ibias_ref, wback_ref,
    next_ref, norm_one_ref, inv_one_ref, low_ref, act_ref, slope_ref, norm_two_ref, inv_two_ref,
    full_ref, acc_ref, *, step,
):
    rows = x_ref.shape[0]
    index = pl.program_id(0)

    @pl.when(index == 0)
    def _():
        for start in range(0, rows, step):
            here = slice(start, start + step)
            total = (
                x_ref[here].astype(f32) + dot(att_ref[here], wout_ref[0]) + lbias_ref[0, 0:1]
            )
            normed, inverse = norm_parts(total)
            full = normed * gains_ref[0, 0:1] + lbias_ref[0, 1:2]
            norm_one_ref[here] = normed.astype(bf16)
            inv_one_ref[here] = jnp.broadcast_to(inverse, (step, LANES))
            low_ref[here] = full.astype(bf16)
            full_ref[here] = full + lbias_ref[0, 2:3]
            acc_ref[here] = jnp.zeros((step, x_ref.shape[1]), f32)

    for start in range(0, rows, step):
        here = slice(start, start + step)
        pre = dot(low_ref[here], win_ref[0]) + ibias_ref[0]
        active, slope = gelu_parts(pre)
        active = active.astype(bf16)
        act_ref[here] = active
        slope_ref[here] = slope.astype(bf16)
        acc_ref[here] += dot(active, wback_ref[0])

    @pl.when(index == pl.num_programs(0) - 1)
    def _():
        for start in range(0, rows, step):
            here = slice(start, start + step)
            normed, inverse = norm_parts(full_ref[here] + acc_ref[here])
            norm_two_ref[here] = normed.astype(bf16)
            inv_two_ref[here] = jnp.broadcast_to(inverse, (step, LANES))
            result = normed * gains_ref[0, 1:2] + lbias_ref[0, 3:4]
            live = jnp.broadcast_to(live_ref[0], result.shape) > 0
            next_ref[here] = jnp.where(live, result, x_ref[here].astype(f32)).astype(next_ref.dtype)


def once(shape, place):
    return pl.BlockSpec(shape, lambda i: place, pipeline_mode=pl.Buffered(1))


def feed(live, x, att, layer, w_out, layer_bias, gains, w_in, in_bias, w_back, kind, block=512):
    rows, model = x.shape
    hidden = w_in.shape[2]
    whole = once((rows, model), (0, 0))
    lanes = once((rows, LANES), (0, 0))
    chunk = pl.BlockSpec((rows, block), lambda i: (0, i))
    return pl.pallas_call(
        functools.partial(feed_kernel, step=row_step(rows)),
        grid=(hidden // block,),
        in_specs=[
            pl.BlockSpec(memory_space=pltpu.SMEM),
            whole,
            whole,
            once((1, model, model), (layer, 0, 0)),
            once((1, 4, model), (layer, 0, 0)),
            once((1, 2, model), (layer, 0, 0)),
            pl.BlockSpec((1, model, block), lambda i: (layer, 0, i)),
            pl.BlockSpec((1, 1, block), lambda i: (layer, 0, i)),
            pl.BlockSpec((1, block, model), lambda i: (layer, i, 0)),
        ],
        out_specs=[whole, whole, lanes, whole, chunk, chunk, whole, lanes],
        out_shape=[
            jax.ShapeDtypeStruct((rows, model), kind),
            jax.ShapeDtypeStruct((rows, model), bf16),
            jax.ShapeDtypeStruct((rows, LANES), f32),
            jax.ShapeDtypeStruct((rows, model), bf16),
            jax.ShapeDtypeStruct((rows, hidden), bf16),
            jax.ShapeDtypeStruct((rows, hidden), bf16),
            jax.ShapeDtypeStruct((rows, model), bf16),
            jax.ShapeDtypeStruct((rows, LANES), f32),
        ],
        scratch_shapes=[pltpu.VMEM((rows, model), f32)] * 2,
        compiler_params=pltpu.CompilerParams(vmem_limit_bytes=56 * MIB),
        name="feed",
    )(live, x, att, w_out, layer_bias, gains, w_in, in_bias.reshape(LAYERS, 1, hidden), w_back)


def norm_back(normed, inverse, grad, gain):
    grad_normed = grad * gain
    mean = jnp.mean(grad_normed, -1, keepdims=True)
    mean_product = jnp.mean(grad_normed * normed, -1, keepdims=True)
    return inverse * (grad_normed - mean - normed * mean_product)


def column_sum(value):
    return jnp.sum(value, 0, keepdims=True)


def feed_back_kernel(
    live_ref, grad_ref, norm_two_ref, inv_two_ref, gains_ref, act_ref, slope_ref, low_ref, win_ref, wback_ref,
    norm_one_ref, inv_one_ref, att_ref, wout_ref,
    sum_one_ref, grad_att_ref, grad_win_ref, grad_wback_ref, grad_wout_ref, small_ref, grad_ibias_ref,
    second_ref, second_low_ref, turned_ref, acc_ref, branch_ref, *, step,
):
    rows = grad_ref.shape[0]
    index = pl.program_id(0)
    starts = range(0, rows, step)

    @pl.when(index == 0)
    def _():
        gain_sum = shift_sum = bias_sum = None
        for start in starts:
            here = slice(start, start + step)
            grad = grad_ref[here].astype(f32)
            through = jnp.where(jnp.broadcast_to(live_ref[0], grad.shape) > 0, grad, 0.0)
            normed = norm_two_ref[here].astype(f32)
            back = norm_back(normed, inv_two_ref[here, 0:1], through, gains_ref[0, 1:2])
            second_ref[here] = back
            second_low_ref[here] = back.astype(bf16)
            acc_ref[here] = jnp.zeros(back.shape, f32)
            terms = (column_sum(through * normed), column_sum(through), column_sum(back))
            gain_sum = terms[0] if gain_sum is None else gain_sum + terms[0]
            shift_sum = terms[1] if shift_sum is None else shift_sum + terms[1]
            bias_sum = terms[2] if bias_sum is None else bias_sum + terms[2]
        small_ref[3:4] = shift_sum
        small_ref[2:3] = bias_sum
        small_ref[5:6] = gain_sum
        small_ref[6:8] = jnp.zeros((2, small_ref.shape[1]), f32)
        turned_ref[...] = low_ref[...].T

    pre_parts = []
    bias_total = None
    for start in starts:
        here = slice(start, start + step)
        grad_pre = dot_nt(second_low_ref[here], wback_ref[0]) * slope_ref[here].astype(f32)
        bias_term = column_sum(grad_pre)
        bias_total = bias_term if bias_total is None else bias_total + bias_term
        pre_low = grad_pre.astype(bf16)
        pre_parts.append(pre_low)
        acc_ref[here] += dot_nt(pre_low, win_ref[0])
    grad_ibias_ref[...] = bias_total
    pre_all = jnp.concatenate(pre_parts, 0)
    grad_win_ref[...] = dot(turned_ref[...], pre_all).astype(bf16)
    grad_wback_ref[...] = dot_tn(act_ref[...], second_low_ref[...]).astype(bf16)

    @pl.when(index == pl.num_programs(0) - 1)
    def _():
        gain_sum = shift_sum = bias_sum = None
        for start in starts:
            here = slice(start, start + step)
            grad_first = second_ref[here] + acc_ref[here]
            normed = norm_one_ref[here].astype(f32)
            back = norm_back(normed, inv_one_ref[here, 0:1], grad_first, gains_ref[0, 0:1])
            sum_one_ref[here] = back
            branch = back.astype(bf16)
            branch_ref[here] = branch
            grad_att_ref[here] = dot_nt(branch, wout_ref[0]).astype(bf16)
            terms = (column_sum(grad_first * normed), column_sum(grad_first), column_sum(back))
            gain_sum = terms[0] if gain_sum is None else gain_sum + terms[0]
            shift_sum = terms[1] if shift_sum is None else shift_sum + terms[1]
            bias_sum = terms[2] if bias_sum is None else bias_sum + terms[2]
        small_ref[1:2] = shift_sum
        small_ref[0:1] = bias_sum
        small_ref[4:5] = gain_sum
        grad_wout_ref[...] = dot_tn(att_ref[...], branch_ref[...]).astype(bf16)


def feed_back(live, grad, saved, att, layer, w_out, gains, w_in, w_back, block=512):
    norm_one, inv_one, low, act, slope, norm_two, inv_two = saved
    rows, model = grad.shape
    hidden = w_in.shape[2]
    whole = once((rows, model), (0, 0))
    lanes = once((rows, LANES), (0, 0))
    square = once((model, model), (0, 0))
    chunk = pl.BlockSpec((rows, block), lambda i: (0, i))
    return pl.pallas_call(
        functools.partial(feed_back_kernel, step=row_step(rows)),
        grid=(hidden // block,),
        in_specs=[
            pl.BlockSpec(memory_space=pltpu.SMEM),
            whole,
            whole,
            lanes,
            once((1, 2, model), (layer, 0, 0)),
            chunk,
            chunk,
            whole,
            pl.BlockSpec((1, model, block), lambda i: (layer, 0, i)),
            pl.BlockSpec((1, block, model), lambda i: (layer, i, 0)),
            whole,
            lanes,
            whole,
            once((1, model, model), (layer, 0, 0)),
        ],
        out_specs=[
            whole,
            whole,
            pl.BlockSpec((model, block), lambda i: (0, i)),
            pl.BlockSpec((block, model), lambda i: (i, 0)),
            square,
            once((8, model), (0, 0)),
            pl.BlockSpec((1, block), lambda i: (0, i)),
        ],
        out_shape=[
            jax.ShapeDtypeStruct((rows, model), f32),
            jax.ShapeDtypeStruct((rows, model), bf16),
            jax.ShapeDtypeStruct((model, hidden), bf16),
            jax.ShapeDtypeStruct((hidden, model), bf16),
            jax.ShapeDtypeStruct((model, model), bf16),
            jax.ShapeDtypeStruct((8, model), f32),
            jax.ShapeDtypeStruct((1, hidden), f32),
        ],
        scratch_shapes=[
            pltpu.VMEM((rows, model), f32),
            pltpu.VMEM((rows, model), bf16),
            pltpu.VMEM((model, rows), bf16),
            pltpu.VMEM((rows, model), f32),
            pltpu.VMEM((rows, model), bf16),
        ],
        compiler_params=pltpu.CompilerParams(vmem_limit_bytes=60 * MIB),
        name="feed_back",
    )(live, grad, norm_two, inv_two, gains, act, slope, low, w_in, w_back, norm_one, inv_one, att, w_out)


def project_back_kernel(
    live_ref, x_ref, gq_ref, gk_ref, gk_far_ref, gv_ref, gv_far_ref, grad_ref, sum_one_ref, w_ref,
    out_ref, grad_w_ref, small_ref, turned_ref, acc_ref, *, step,
):
    rows = x_ref.shape[0]
    index = pl.program_id(0)

    @pl.when(index == 0)
    def _():
        turned_ref[...] = x_ref[...].astype(bf16).T
        for start in range(0, rows, step):
            here = slice(start, start + step)
            grad = grad_ref[here].astype(f32)
            skipped = jnp.where(jnp.broadcast_to(live_ref[0], grad.shape) > 0, 0.0, grad)
            acc_ref[here] = skipped + sum_one_ref[here]

    def consume(grad_part):
        low = grad_part.astype(bf16)
        small_ref[...] = column_sum(grad_part)
        grad_w_ref[...] = dot(turned_ref[...], low).astype(bf16)
        for start in range(0, rows, step):
            here = slice(start, start + step)
            acc_ref[here] += dot_nt(low[here], w_ref[0])

    third = pl.num_programs(0) // 3

    @pl.when(index < third)
    def _():
        consume(gq_ref[...].astype(f32))

    @pl.when((index >= third) & (index < 2 * third))
    def _():
        consume(gk_ref[...].astype(f32) + gk_far_ref[...].astype(f32))

    @pl.when(index >= 2 * third)
    def _():
        consume(gv_ref[...].astype(f32) + gv_far_ref[...].astype(f32))

    @pl.when(index == pl.num_programs(0) - 1)
    def _():
        out_ref[...] = acc_ref[...].astype(out_ref.dtype)


def project_back(live, x, gq, gk, gk_far, gv, gv_far, grad, sum_one, w_qkv, layer, kind, block=256):
    rows, model = x.shape
    width = w_qkv.shape[2]
    third = model // block
    whole = once((rows, model), (0, 0))

    def part(which):
        return pl.BlockSpec((rows, block), lambda i: (0, jnp.clip(i - which * third, 0, third - 1)))

    return pl.pallas_call(
        functools.partial(project_back_kernel, step=row_step(rows)),
        grid=(width // block,),
        in_specs=[
            pl.BlockSpec(memory_space=pltpu.SMEM),
            whole,
            part(0),
            part(1),
            part(1),
            part(2),
            part(2),
            whole,
            whole,
            pl.BlockSpec((1, model, block), lambda i: (layer, 0, i)),
        ],
        out_specs=[
            whole,
            pl.BlockSpec((model, block), lambda i: (0, i)),
            pl.BlockSpec((1, block), lambda i: (0, i)),
        ],
        out_shape=[
            jax.ShapeDtypeStruct((rows, model), kind),
            jax.ShapeDtypeStruct((model, width), bf16),
            jax.ShapeDtypeStruct((1, width), f32),
        ],
        scratch_shapes=[pltpu.VMEM((model, rows), bf16), pltpu.VMEM((rows, model), f32)],
        compiler_params=pltpu.CompilerParams(vmem_limit_bytes=56 * MIB),
        name="project_back",
    )(live, x, gq, gk, gk_far, gv, gv_far, grad, sum_one, w_qkv)


def body(sizes, frames, lengths, drop_bits, w_qkv, attn_bias, w_out, layer_bias, gains, w_in, in_bias, w_back, cotangent):
    seq_size, utt_size = sizes
    half = seq_size // 2
    utt_count, block_rows, model = frames.shape
    place = lax.axis_index("seq")
    mine = place // half
    partner = (place + half) % seq_size
    swap = [(i, (i + half) % seq_size) for i in range(seq_size)]
    groups = [list(range(half)), list(range(half, seq_size))]

    def pick(array, index):
        return lax.dynamic_index_in_dim(array, index, 0, keepdims=False)

    def to_whole(array):
        far = lax.ppermute(pick(array, 1 - mine), "seq", swap)
        return jnp.concatenate([pick(array, mine), far], 0)

    def to_split(array):
        near, far = array[:block_rows], lax.ppermute(array[block_rows:], "seq", swap)
        first = jnp.where(mine == 0, near, far)
        second = jnp.where(mine == 0, far, near)
        return jnp.stack([first, second])

    length = pick(lengths, mine).reshape(1)
    live_bits = pick(drop_bits, mine)
    members = mine * half + jnp.arange(half, dtype=jnp.int32)
    if half == 2:
        other = mine * half + (1 - place % half)
        members = jnp.stack([place, other])
    base = jnp.stack([members, (members + half) % seq_size], 1).reshape(-1).astype(jnp.int32) * block_rows
    rows = 2 * block_rows
    pair = [(i, i ^ 1) for i in range(seq_size)]
    bias = jnp.concatenate([attn_bias[:, 0], jnp.zeros_like(attn_bias[:, 0]), attn_bias[:, 1]], 1)
    scale = jnp.concatenate([jnp.full((1, model), LOG2E * HEAD_DIM**-0.5, f32), jnp.ones((1, 2 * model), f32)], 1)

    x = to_whole(frames)
    saved_all = []
    for layer in range(LAYERS):
        live = live_bits[layer].reshape(1)
        kv = project(x, w_qkv, layer, bias[layer : layer + 1], scale, model, 2 * model)
        if half == 2:
            key_values = [kv, lax.ppermute(kv, "seq", pair)]
        else:
            key_values = [lax.all_gather(kv, "seq", axis=0, tiled=True, axis_index_groups=groups)]
        q = project(x, w_qkv, layer, bias[layer : layer + 1], scale, 0, model)
        att, extra = attend(length, base, q, key_values, block_rows)
        kind = f32 if layer + 1 < LAYERS else bf16
        nxt, *saved = feed(live, x, att, layer, w_out, layer_bias, gains, w_in, in_bias, w_back, kind)
        saved_all.append((x, q, key_values, att, extra, saved, live))
        x = nxt
    mixed = to_split(x)

    grad = to_whole(cotangent)
    outputs = [None] * LAYERS
    smalls = [None] * LAYERS
    for layer in reversed(range(LAYERS)):
        x, q, key_values, att, extra, saved, live = saved_all[layer]
        sum_one, grad_att, grad_win, grad_wback, grad_wout, small, grad_ibias = feed_back(
            live, grad, saved, att, layer, w_out, gains, w_in, w_back
        )
        back = attend_back(length, base, q, grad_att, att, extra, key_values, block_rows)
        gq = back[0]
        parts = len(key_values)
        if half == 2:
            gk, gk_send, gv, gv_send = back[1:]
            gk_far = lax.ppermute(gk_send, "seq", pair)
            gv_far = lax.ppermute(gv_send, "seq", pair)
        else:
            gk, gv = (
                lax.psum_scatter(part, "seq", scatter_dimension=0, tiled=True, axis_index_groups=groups)
                for part in back[1:]
            )
            gk_far, gv_far = jnp.zeros_like(gk), jnp.zeros_like(gv)
        kind = f32 if layer > 0 else bf16
        grad, grad_wqkv, sums = project_back(live, x, gq, gk, gk_far, gv, gv_far, grad, sum_one, w_qkv, layer, kind)
        wide = jnp.concatenate(
            [
                grad_wqkv,
                grad_wout,
                grad_win,
                grad_wback.reshape(utt_size, 4, model // utt_size, model).transpose(0, 2, 1, 3).reshape(model, 4 * model),
            ],
            1,
        )
        bit = 1
        while bit < seq_size:
            columns = wide.shape[1] // 2
            upper = (place // bit) % 2
            keep = lax.dynamic_slice_in_dim(wide, upper * columns, columns, 1)
            send = lax.dynamic_slice_in_dim(wide, (1 - upper) * columns, columns, 1)
            wide = keep + lax.ppermute(send, "seq", [(i, i ^ bit) for i in range(seq_size)])
            bit *= 2
        wide = lax.psum_scatter(wide, "utt", scatter_dimension=0, tiled=True)
        whole = lax.all_gather(wide, "seq", axis=0, tiled=False)
        order = []
        for piece in range(seq_size):
            device, left, width, bit = 0, piece, seq_size, 1
            while bit < seq_size:
                width //= 2
                if left >= width:
                    device += bit
                    left -= width
                bit *= 2
            order.append(device)
        wide = jnp.concatenate([whole[device] for device in order], 1).astype(f32)
        outputs[layer] = (
            wide[:, : 3 * model],
            wide[:, 3 * model : 4 * model],
            wide[:, 4 * model : 8 * model],
            wide[:, 8 * model :].reshape(-1, 4, model).transpose(1, 0, 2).reshape(-1, model),
        )
        sums = sums.reshape(3, model)
        smalls[layer] = jnp.concatenate(
            [small[:6], sums[0:1], sums[2:3], grad_ibias.reshape(4, model)], 0
        )
    grad_frames = to_split(grad)
    small = lax.psum(jnp.stack(smalls), ("utt", "seq"))
    unit = model // utt_size
    at = lax.axis_index("utt") * unit
    mine_small = lax.dynamic_slice_in_dim(small[:, :8], at, unit, 2)
    ibias = lax.dynamic_slice_in_dim(small[:, 8:].reshape(LAYERS, 4 * model), 4 * at, 4 * unit, 1)
    stacked = [jnp.stack([per[member] for per in outputs]) for member in range(4)]
    return (
        mixed,
        grad_frames,
        stacked[0],
        mine_small[:, 6:8],
        stacked[1],
        mine_small[:, 0:4],
        mine_small[:, 4:6],
        stacked[2],
        ibias,
        stacked[3],
    )


def solution(mesh):
    frame_spec = P("utt", "seq", None)
    sizes = (mesh.shape["seq"], mesh.shape["utt"])
    return jax.shard_map(
        functools.partial(body, sizes),
        mesh=mesh,
        in_specs=(frame_spec, P("utt"), P("utt", None)) + (P(),) * 8 + (frame_spec,),
        out_specs=(
            frame_spec,
            frame_spec,
            P(None, "utt", None),
            P(None, None, "utt"),
            P(None, "utt", None),
            P(None, None, "utt"),
            P(None, None, "utt"),
            P(None, "utt", None),
            P(None, "utt"),
            P(None, "utt", None),
        ),
        check_vma=False,
    )
```

```python
import functools

import jax
import jax.numpy as jnp
from jax import lax
from jax.experimental import pallas as pl
from jax.experimental.pallas import tpu as pltpu
from jax.sharding import PartitionSpec as P

HEADS = 12
HEAD_DIM = 64
LAYERS = 2
LOG2E = 1.4426950408889634
LN2 = 0.6931471805599453
MASKED = -1e30
LANES = 128
MIB = 1 << 20

bf16 = jnp.bfloat16
f32 = jnp.float32


def dot(left, right):
    return jnp.dot(left, right, preferred_element_type=f32)


def dot_nt(left, right):
    return lax.dot_general(left, right, (((1,), (1,)), ((), ())), preferred_element_type=f32)


def dot_tn(left, right):
    return lax.dot_general(left, right, (((0,), (0,)), ((), ())), preferred_element_type=f32)


def row_step(rows):
    for step in (256, 192, 128, 96, 64, 32, 16):
        if rows % step == 0:
            return step
    return rows


def project_kernel(x_ref, w_ref, bias_ref, scale_ref, out_ref):
    low = x_ref[...].astype(bf16)
    out_ref[...] = ((dot(low, w_ref[0]) + bias_ref[...]) * scale_ref[...]).astype(bf16)


def project(x, w_qkv, layer, bias, scale, first, width, block=256):
    rows, model = x.shape
    return pl.pallas_call(
        project_kernel,
        grid=(width // block,),
        in_specs=[
            pl.BlockSpec((rows, model), lambda i: (0, 0)),
            pl.BlockSpec((1, model, block), lambda i: (layer, 0, i + first // block)),
            pl.BlockSpec((1, block), lambda i: (0, i + first // block)),
            pl.BlockSpec((1, block), lambda i: (0, i + first // block)),
        ],
        out_specs=pl.BlockSpec((rows, block), lambda i: (0, i)),
        out_shape=jax.ShapeDtypeStruct((rows, width), bf16),
        compiler_params=pltpu.CompilerParams(vmem_limit_bytes=40 * MIB),
        name="project",
    )(x, w_qkv, bias, scale)


def lane_index():
    return lax.broadcasted_iota(jnp.int32, (1, LANES), 1)


def head_lanes(head):
    lane = lane_index()
    own = (lane < HEAD_DIM) if head == 0 else (lane >= HEAD_DIM)
    return jnp.where(own, 1.0, 0.0).astype(bf16), jnp.where(own, 0.0, 1.0).astype(bf16)


def fill_key_columns(length_ref, base_ref, columns_ref, block_rows):
    @pl.when(pl.program_id(0) == 0)
    def _():
        for block in range(columns_ref.shape[0] // block_rows):
            row = lax.broadcasted_iota(jnp.int32, (block_rows, LANES), 0) + base_ref[block]
            slot = lax.broadcasted_iota(jnp.int32, (block_rows, LANES), 1) & (HEAD_DIM - 1)
            mask = jnp.where(row < length_ref[0], 0.0, MASKED)
            column = jnp.where(slot == 3, mask, jnp.where(slot < 3, 1.0, 0.0))
            columns_ref[block * block_rows : (block + 1) * block_rows] = column.astype(bf16)


def split_parts(value, last):
    slot = lane_index() & (HEAD_DIM - 1)
    high = value.astype(bf16).astype(f32)
    rest = value - high
    middle = rest.astype(bf16).astype(f32)
    low = rest - middle
    tail = jnp.where(slot == 2, low, jnp.where(slot == 3, last, 0.0))
    return jnp.where(slot == 0, high, jnp.where(slot == 1, middle, tail)).astype(bf16)


def attend_kernel(length_ref, base_ref, q_ref, *refs, parts, block_rows, step):
    key_refs = refs[:parts]
    value_refs = refs[parts : 2 * parts]
    out_ref, extra_ref, columns_ref = refs[2 * parts :]
    rows = q_ref.shape[0]
    fill_key_columns(length_ref, base_ref, columns_ref, block_rows)
    lane = lane_index()
    slot = lane & (HEAD_DIM - 1)

    def operands(head):
        own, other = head_lanes(head)
        constant = jnp.where(slot == 3, 1.0, 0.0).astype(bf16) * other
        keys, values = [], []
        offset = 0
        for key_ref, value_ref in zip(key_refs, value_refs):
            size = key_ref.shape[0]
            keys.append(key_ref[...] * own + columns_ref[offset : offset + size] * other)
            values.append(value_ref[...] * own + other)
            offset += size
        return own, constant, keys, values

    def finish(start, size, sums, shifts):
        top = jnp.where(lane < HEAD_DIM, sums[0], sums[1])
        total = jnp.where(lane < HEAD_DIM, sums[1], sums[0])
        out_ref[pl.ds(start, size)] = (top / pltpu.roll(total, HEAD_DIM, 1)).astype(bf16)
        log_total = jnp.log2(total)
        if shifts is not None:
            log_total = log_total + jnp.where(lane < HEAD_DIM, shifts[1], shifts[0])
        extra_ref[pl.ds(start, size)] = split_parts(-log_total, 1.0)
        return total

    all_sums = []
    for head in range(2):
        own, constant, keys, values = operands(head)
        sums = []
        for start in range(0, rows, step):
            query = q_ref[start : start + step] * own + constant
            total = None
            for key, value in zip(keys, values):
                probs = jnp.exp2(dot_nt(query, key)).astype(bf16)
                term = dot(probs, value)
                total = term if total is None else total + term
            sums.append(total)
        all_sums.append(sums)
    bad = jnp.float32(0.0)
    for index, start in enumerate(range(0, rows, step)):
        total = finish(start, step, (all_sums[0][index], all_sums[1][index]), None)
        inside = (total > 2.0**-80) & (total < 2.0**100)
        bad = bad + jnp.sum(jnp.where(inside, 0.0, 1.0))

    @pl.when(bad > 0.0)
    def _():
        size = 16

        def body(index, carry):
            start = pl.multiple_of(index * size, size)
            sums, shifts = [], []
            for head in range(2):
                own, constant, keys, values = operands(head)
                query = q_ref[pl.ds(start, size)] * own + constant
                scores = [dot_nt(query, key) for key in keys]
                largest = functools.reduce(
                    jnp.maximum, [jnp.max(part, -1, keepdims=True) for part in scores]
                )
                total = None
                for part, value in zip(scores, values):
                    term = dot(jnp.exp2(part - largest).astype(bf16), value)
                    total = term if total is None else total + term
                sums.append(total)
                shifts.append(largest)
            finish(start, size, sums, shifts)
            return carry

        lax.fori_loop(0, rows // size, body, 0)


def attend(length, base, q, key_values, block_rows):
    rows, model = q.shape
    pairs = model // LANES
    parts = len(key_values)
    total = sum(part.shape[0] for part in key_values)
    scalar = pl.BlockSpec(memory_space=pltpu.SMEM)

    def column(size, shift=0):
        return pl.BlockSpec((size, LANES), lambda i: (0, i + shift))

    kernel = functools.partial(
        attend_kernel, parts=parts, block_rows=block_rows, step=row_step(rows)
    )
    return pl.pallas_call(
        kernel,
        grid=(pairs,),
        in_specs=[scalar, scalar, column(rows)]
        + [column(part.shape[0]) for part in key_values]
        + [column(part.shape[0], pairs) for part in key_values],
        out_specs=[column(rows), column(rows)],
        out_shape=[jax.ShapeDtypeStruct((rows, model), bf16)] * 2,
        scratch_shapes=[pltpu.VMEM((total, LANES), bf16)],
        compiler_params=pltpu.CompilerParams(vmem_limit_bytes=56 * MIB),
        name="attend",
    )(length, base, q, *key_values, *key_values)


def attend_back_kernel(
    length_ref, base_ref, core_ref, q_ref, grad_ref, out_ref, extra_ref, *refs, parts, block_rows, step
):
    key_refs = refs[:parts]
    value_refs = refs[parts : 2 * parts]
    grad_query_ref, bias_ref = refs[2 * parts : 2 * parts + 2]
    grad_refs = refs[2 * parts + 2 : 3 * parts + 2]
    half_ref = refs[3 * parts + 2] if parts == 2 else None
    columns_ref = refs[-1]
    rows = q_ref.shape[0]
    fill_key_columns(length_ref, base_ref, columns_ref, block_rows)
    lane = lane_index()
    slot = lane & (HEAD_DIM - 1)
    value_column = jnp.where(slot < 3, 1.0, 0.0).astype(bf16)
    from_lane = lax.broadcasted_iota(jnp.int32, (LANES, LANES), 0)
    to_lane = lax.broadcasted_iota(jnp.int32, (LANES, LANES), 1)
    swap = jnp.where((from_lane < HEAD_DIM) != (to_lane < HEAD_DIM), -1.0, 0.0).astype(bf16)
    grad_keys = [None] * parts
    grad_values = [None] * parts
    heads = [head_lanes(head) for head in range(2)]
    offsets = []
    offset = 0
    for part in range(parts):
        offsets.append(offset)
        offset += key_refs[part].shape[0]

    def add(old, new):
        return new if old is None else old + new

    query_sum = None
    for start in range(0, rows, step):
        query, grad = q_ref[start : start + step], grad_ref[start : start + step]
        extra = extra_ref[start : start + step]
        product = grad.astype(f32) * out_ref[start : start + step].astype(f32)
        high = product.astype(bf16)
        low = (product - high.astype(f32)).astype(bf16)
        inner = split_parts(dot(high, swap) + dot(low, swap), 0.0)
        grad_query = None
        for head in range(2):
            own, other = heads[head]
            query_own, grad_own = query * own, grad * own
            query_full, grad_full = query_own + extra * other, grad_own + inner * other
            query_turned, grad_turned = query_own.T, grad_own.T
            for part in range(parts):
                size = key_refs[part].shape[0]
                key_own = key_refs[part][...] * own
                key_full = key_own + columns_ref[offsets[part] : offsets[part] + size] * other
                value_full = value_refs[part][...] * own + value_column * other
                probs = jnp.exp2(dot_nt(query_full, key_full))
                grad_scores = (probs * dot_nt(grad_full, value_full)).astype(bf16)
                grad_values[part] = add(grad_values[part], dot(grad_turned, probs.astype(bf16)))
                grad_keys[part] = add(grad_keys[part], dot(query_turned, grad_scores))
                grad_query = add(grad_query, dot(grad_scores, key_own))
        grad_query = grad_query * HEAD_DIM**-0.5
        query_sum = add(query_sum, column_sum(grad_query))
        grad_query_ref[start : start + step] = grad_query.astype(bf16)
    value_sum = None
    for part in range(parts):
        grad_value = grad_values[part].T
        value_sum = add(value_sum, column_sum(grad_value))
        grad_refs[part][0] = (grad_keys[part] * LN2).T.astype(bf16)
        grad_refs[part][1] = grad_value.astype(bf16)
    bias_ref[0:1] = query_sum
    bias_ref[1:2] = value_sum
    bias_ref[2:8] = jnp.zeros((6, LANES), f32)
    if half_ref is not None:
        first = (1 - core_ref[0]) * (pl.num_programs(0) // 2)
        index = pl.program_id(0)

        @pl.when((index >= first) & (index < first + pl.num_programs(0) // 2))
        def _():
            half_ref[0] = grad_query_ref[...]
            half_ref[1] = grad_refs[0][0]
            half_ref[2] = grad_refs[0][1]


def attend_back(length, base, core, q, grad, out, extra, key_values, block_rows):
    rows, model = q.shape
    pairs = model // LANES
    parts = len(key_values)
    sizes = [part.shape[0] for part in key_values]

    def column(size, shift=0):
        return pl.BlockSpec((size, LANES), lambda i, *_: (0, i + shift))

    def stack(count, size):
        return pl.BlockSpec((count, size, LANES), lambda i, *_: (0, 0, i))

    def half_place(i, length, base, core):
        return 0, 0, jnp.clip(i - (1 - core[0]) * (pairs // 2), 0, pairs // 2 - 1)

    kernel = functools.partial(
        attend_back_kernel, parts=parts, block_rows=block_rows, step=row_step(rows)
    )
    out_specs = [column(rows), pl.BlockSpec((8, LANES), lambda i, *_: (0, i))]
    out_specs += [stack(2, size) for size in sizes]
    out_shape = [jax.ShapeDtypeStruct((rows, model), bf16), jax.ShapeDtypeStruct((8, model), f32)]
    out_shape += [jax.ShapeDtypeStruct((2, size, model), bf16) for size in sizes]
    if parts == 2:
        out_specs.append(pl.BlockSpec((3, rows, LANES), half_place))
        out_shape.append(jax.ShapeDtypeStruct((3, rows, model // 2), bf16))
    return pl.pallas_call(
        kernel,
        grid_spec=pltpu.PrefetchScalarGridSpec(
            num_scalar_prefetch=3,
            grid=(pairs,),
            in_specs=[column(rows)] * 4
            + [column(size) for size in sizes]
            + [column(size, pairs) for size in sizes],
            out_specs=out_specs,
            scratch_shapes=[pltpu.VMEM((sum(sizes), LANES), bf16)],
        ),
        out_shape=out_shape,
        compiler_params=pltpu.CompilerParams(vmem_limit_bytes=60 * MIB),
        name="attend_back",
    )(length, base, core, q, grad, out, extra, *key_values, *key_values)


def norm_parts(value):
    mean = jnp.mean(value, -1, keepdims=True)
    centred = value - mean
    inverse = lax.rsqrt(jnp.mean(centred * centred, -1, keepdims=True) + 1e-05)
    return centred * inverse, inverse


def gelu_parts(pre):
    size = jnp.abs(pre)
    ratio = 1.0 / (1.0 + size * (0.3275911 * 0.7071067811865476))
    poly = 1.061405429 * ratio - 1.453152027
    poly = poly * ratio + 1.421413741
    poly = poly * ratio - 0.284496736
    poly = (poly * ratio + 0.254829592) * ratio
    bell = jnp.exp2(pre * pre * (-0.5 * LOG2E))
    tail = 0.5 * poly * bell
    share = jnp.where(pre < 0.0, tail, 1.0 - tail)
    return pre * share, share + pre * bell * 0.3989422804014327


def feed_kernel(
    live_ref, x_ref, att_ref, wout_ref, lbias_ref, gains_ref, win_ref, ibias_ref, wback_ref,
    next_ref, next_low_ref, norm_one_ref, inv_one_ref, low_ref, act_ref, slope_ref, norm_two_ref, inv_two_ref,
    full_ref, acc_ref, *, step,
):
    rows = x_ref.shape[0]
    index = pl.program_id(0)

    @pl.when(index == 0)
    def _():
        for start in range(0, rows, step):
            here = slice(start, start + step)
            total = (
                x_ref[here].astype(f32) + dot(att_ref[here], wout_ref[0]) + lbias_ref[0, 0:1]
            )
            normed, inverse = norm_parts(total)
            full = normed * gains_ref[0, 0:1] + lbias_ref[0, 1:2]
            norm_one_ref[here] = normed.astype(bf16)
            inv_one_ref[here] = jnp.broadcast_to(inverse, (step, LANES))
            low_ref[here] = full.astype(bf16)
            full_ref[here] = full + lbias_ref[0, 2:3]
            acc_ref[here] = jnp.zeros((step, x_ref.shape[1]), f32)

    for start in range(0, rows, step):
        here = slice(start, start + step)
        pre = dot(low_ref[here], win_ref[0]) + ibias_ref[0]
        active, slope = gelu_parts(pre)
        active = active.astype(bf16)
        act_ref[here] = active
        slope_ref[here] = slope.astype(bf16)
        acc_ref[here] += dot(active, wback_ref[0])

    @pl.when(index == pl.num_programs(0) - 1)
    def _():
        for start in range(0, rows, step):
            here = slice(start, start + step)
            normed, inverse = norm_parts(full_ref[here] + acc_ref[here])
            norm_two_ref[here] = normed.astype(bf16)
            inv_two_ref[here] = jnp.broadcast_to(inverse, (step, LANES))
            result = normed * gains_ref[0, 1:2] + lbias_ref[0, 3:4]
            live = jnp.broadcast_to(live_ref[0], result.shape) > 0
            result = jnp.where(live, result, x_ref[here].astype(f32))
            next_ref[here] = result
            next_low_ref[here] = result.astype(bf16)


def once(shape, place):
    return pl.BlockSpec(shape, lambda i: place, pipeline_mode=pl.Buffered(1))


def feed(live, x, att, layer, w_out, layer_bias, gains, w_in, in_bias, w_back, block=512):
    rows, model = x.shape
    hidden = w_in.shape[2]
    whole = once((rows, model), (0, 0))
    lanes = once((rows, LANES), (0, 0))
    chunk = pl.BlockSpec((rows, block), lambda i: (0, i))
    return pl.pallas_call(
        functools.partial(feed_kernel, step=row_step(rows)),
        grid=(hidden // block,),
        in_specs=[
            pl.BlockSpec(memory_space=pltpu.SMEM),
            whole,
            whole,
            once((1, model, model), (layer, 0, 0)),
            once((1, 4, model), (layer, 0, 0)),
            once((1, 2, model), (layer, 0, 0)),
            pl.BlockSpec((1, model, block), lambda i: (layer, 0, i)),
            pl.BlockSpec((1, 1, block), lambda i: (layer, 0, i)),
            pl.BlockSpec((1, block, model), lambda i: (layer, i, 0)),
        ],
        out_specs=[whole, whole, whole, lanes, whole, chunk, chunk, whole, lanes],
        out_shape=[
            jax.ShapeDtypeStruct((rows, model), f32),
            jax.ShapeDtypeStruct((rows, model), bf16),
            jax.ShapeDtypeStruct((rows, model), bf16),
            jax.ShapeDtypeStruct((rows, LANES), f32),
            jax.ShapeDtypeStruct((rows, model), bf16),
            jax.ShapeDtypeStruct((rows, hidden), bf16),
            jax.ShapeDtypeStruct((rows, hidden), bf16),
            jax.ShapeDtypeStruct((rows, model), bf16),
            jax.ShapeDtypeStruct((rows, LANES), f32),
        ],
        scratch_shapes=[pltpu.VMEM((rows, model), f32)] * 2,
        compiler_params=pltpu.CompilerParams(vmem_limit_bytes=56 * MIB),
        name="feed",
    )(live, x, att, w_out, layer_bias, gains, w_in, in_bias.reshape(LAYERS, 1, hidden), w_back)


def norm_back(normed, inverse, grad, gain):
    grad_normed = grad * gain
    mean = jnp.mean(grad_normed, -1, keepdims=True)
    mean_product = jnp.mean(grad_normed * normed, -1, keepdims=True)
    return inverse * (grad_normed - mean - normed * mean_product)


def column_sum(value):
    return jnp.sum(value, 0, keepdims=True)


def feed_back_kernel(
    live_ref, core_ref, grad_ref, norm_two_ref, inv_two_ref, gains_ref, slope_ref, win_ref, wback_ref,
    norm_one_ref, inv_one_ref, wout_ref,
    sum_one_ref, grad_att_ref, pre_ref, pre_send_ref, second_low_ref, branch_ref, send_ref, small_ref, grad_ibias_ref,
    second_ref, acc_ref, *, step,
):
    rows, model = grad_ref.shape
    index = pl.program_id(0)
    count = pl.num_programs(0)
    starts = range(0, rows, step)
    far = pl.multiple_of((1 - core_ref[0]) * (model // 2), LANES)

    def add(old, new):
        return new if old is None else old + new

    @pl.when(index == 0)
    def _():
        gain_sum = shift_sum = bias_sum = None
        for start in starts:
            here = slice(start, start + step)
            grad = grad_ref[here].astype(f32)
            through = jnp.where(jnp.broadcast_to(live_ref[0], grad.shape) > 0, grad, 0.0)
            normed = norm_two_ref[here].astype(f32)
            back = norm_back(normed, inv_two_ref[here, 0:1], through, gains_ref[0, 1:2])
            second_ref[here] = back
            second_low_ref[here] = back.astype(bf16)
            acc_ref[here] = jnp.zeros(back.shape, f32)
            gain_sum = add(gain_sum, column_sum(through * normed))
            shift_sum = add(shift_sum, column_sum(through))
            bias_sum = add(bias_sum, column_sum(back))
        small_ref[3:4] = shift_sum
        small_ref[2:3] = bias_sum
        small_ref[5:6] = gain_sum
        small_ref[6:8] = jnp.zeros((2, model), f32)
        send_ref[:, : model // 2] = second_low_ref[:, pl.ds(far, model // 2)]

    bias_total = None
    for start in starts:
        here = slice(start, start + step)
        grad_pre = dot_nt(second_low_ref[here], wback_ref[0]) * slope_ref[here].astype(f32)
        bias_total = add(bias_total, column_sum(grad_pre))
        pre_low = grad_pre.astype(bf16)
        pre_ref[here] = pre_low
        acc_ref[here] += dot_nt(pre_low, win_ref[0])
    grad_ibias_ref[...] = bias_total
    first = (1 - core_ref[0]) * (count // 2)

    @pl.when((index >= first) & (index < first + count // 2))
    def _():
        pre_send_ref[...] = pre_ref[...]

    @pl.when(index == count - 1)
    def _():
        gain_sum = shift_sum = bias_sum = None
        for start in starts:
            here = slice(start, start + step)
            grad_first = second_ref[here] + acc_ref[here]
            normed = norm_one_ref[here].astype(f32)
            back = norm_back(normed, inv_one_ref[here, 0:1], grad_first, gains_ref[0, 0:1])
            sum_one_ref[here] = back
            branch = back.astype(bf16)
            branch_ref[here] = branch
            grad_att_ref[here] = dot_nt(branch, wout_ref[0]).astype(bf16)
            gain_sum = add(gain_sum, column_sum(grad_first * normed))
            shift_sum = add(shift_sum, column_sum(grad_first))
            bias_sum = add(bias_sum, column_sum(back))
        small_ref[1:2] = shift_sum
        small_ref[0:1] = bias_sum
        small_ref[4:5] = gain_sum
        send_ref[:, model // 2 :] = branch_ref[:, pl.ds(far, model // 2)]


def feed_back(live, core, grad, saved, layer, w_out, gains, w_in, w_back, block=512):
    norm_one, inv_one, low, act, slope, norm_two, inv_two = saved
    rows, model = grad.shape
    hidden = w_in.shape[2]
    count = hidden // block

    def fixed(shape, place):
        return pl.BlockSpec(shape, lambda i, *_: place, pipeline_mode=pl.Buffered(1))

    whole = fixed((rows, model), (0, 0))
    lanes = fixed((rows, LANES), (0, 0))
    chunk = pl.BlockSpec((rows, block), lambda i, *_: (0, i))

    def half_place(i, live, core):
        return 0, jnp.clip(i - (1 - core[0]) * (count // 2), 0, count // 2 - 1)

    return pl.pallas_call(
        functools.partial(feed_back_kernel, step=row_step(rows)),
        grid_spec=pltpu.PrefetchScalarGridSpec(
            num_scalar_prefetch=2,
            grid=(count,),
            in_specs=[
                whole,
                whole,
                lanes,
                fixed((1, 2, model), (layer, 0, 0)),
                chunk,
                pl.BlockSpec((1, model, block), lambda i, *_: (layer, 0, i)),
                pl.BlockSpec((1, block, model), lambda i, *_: (layer, i, 0)),
                whole,
                lanes,
                fixed((1, model, model), (layer, 0, 0)),
            ],
            out_specs=[
                whole,
                whole,
                chunk,
                pl.BlockSpec((rows, block), half_place),
                whole,
                whole,
                whole,
                fixed((8, model), (0, 0)),
                pl.BlockSpec((1, block), lambda i, *_: (0, i)),
            ],
            scratch_shapes=[pltpu.VMEM((rows, model), f32)] * 2,
        ),
        out_shape=[
            jax.ShapeDtypeStruct((rows, model), f32),
            jax.ShapeDtypeStruct((rows, model), bf16),
            jax.ShapeDtypeStruct((rows, hidden), bf16),
            jax.ShapeDtypeStruct((rows, hidden // 2), bf16),
            jax.ShapeDtypeStruct((rows, model), bf16),
            jax.ShapeDtypeStruct((rows, model), bf16),
            jax.ShapeDtypeStruct((rows, model), bf16),
            jax.ShapeDtypeStruct((8, model), f32),
            jax.ShapeDtypeStruct((1, hidden), f32),
        ],
        compiler_params=pltpu.CompilerParams(vmem_limit_bytes=60 * MIB),
        name="feed_back",
    )(live, core, grad, norm_two, inv_two, gains, slope, w_in, w_back, norm_one, inv_one, w_out)


def project_back_kernel(live_ref, gq_ref, gkv_ref, far_ref, grad_ref, sum_one_ref, w_ref, out_ref, acc_ref, *, step):
    index = pl.program_id(0)
    rows = gq_ref.shape[0]

    for start in range(0, rows, step):
        here = slice(start, start + step)

        @pl.when(index == 0)
        def _():
            grad = grad_ref[here].astype(f32)
            skipped = jnp.where(jnp.broadcast_to(live_ref[0], grad.shape) > 0, 0.0, grad)
            acc_ref[here] = skipped + sum_one_ref[here] + dot_nt(gq_ref[here], w_ref[0])

        @pl.when(index > 0)
        def _():
            total = (gkv_ref[0, here].astype(f32) + far_ref[0, here].astype(f32)).astype(bf16)
            acc_ref[here] += dot_nt(total, w_ref[0])

    @pl.when(index == pl.num_programs(0) - 1)
    def _():
        out_ref[...] = acc_ref[...].astype(out_ref.dtype)


def project_back(live, gq, gkv, far, grad, sum_one, w_qkv, layer, kind):
    rows, model = gq.shape
    whole = once((rows, model), (0, 0))
    part = pl.BlockSpec((1, rows, model), lambda i: (jnp.maximum(i - 1, 0), 0, 0))
    return pl.pallas_call(
        functools.partial(project_back_kernel, step=row_step(rows)),
        grid=(3,),
        in_specs=[
            pl.BlockSpec(memory_space=pltpu.SMEM),
            whole,
            part,
            part,
            whole,
            whole,
            pl.BlockSpec((1, model, model), lambda i: (layer, 0, i)),
        ],
        out_specs=whole,
        out_shape=jax.ShapeDtypeStruct((rows, model), kind),
        scratch_shapes=[pltpu.VMEM((rows, model), f32)],
        compiler_params=pltpu.CompilerParams(vmem_limit_bytes=56 * MIB),
        name="project_back",
    )(live, gq, gkv, far, grad, sum_one, w_qkv)


def grads_kernel(where_ref, *refs, with_feed, with_project):
    refs = list(refs)
    if with_feed:
        low, low_far, pre, pre_far, att, att_far, branch, act, act_far, second, send_far = refs[:11]
        del refs[:11]
    if with_project:
        x, x_far, gq, gkv, gkv_far, gkv_send, half_far = refs[:7]
        del refs[:7]
    a_keep, a_send, b_keep, b_send = refs[:4]
    step = pl.program_id(0)
    mine = where_ref[2]
    unit = a_keep.shape[3]
    utts = 8

    def store_first(ref, value, offset):
        for u in range(utts):
            ref[u % 2, u // 2 % 2, u // 4, :, offset : offset + value.shape[1]] = value[u * unit : (u + 1) * unit]

    def store_second(u, value, offset):
        for parity in range(2):

            @pl.when(mine == parity)
            def _():
                ref = b_keep if u % 2 == parity else b_send
                ref[u // 2 % 2, u // 4, :, offset : offset + value.shape[1]] = value

    def half(ref):
        return ref[...]

    if with_feed:
        model = low.shape[1]

        @pl.when(step <= 1)
        def _():
            value = (dot_tn(low[...], pre[...]) + dot_tn(low_far[...], pre_far[...])).astype(bf16)

            @pl.when(step == 0)
            def _():
                store_first(a_send, value, 0)

            @pl.when(step == 1)
            def _():
                store_first(a_keep, value, 0)

        @pl.when(step == 1)
        def _():
            value = (
                dot_tn(att[...], branch[...]) + dot_tn(att_far[...], send_far[:, model // 2 :])
            ).astype(bf16)
            for u in range(utts):
                store_second(u, value[u * unit : (u + 1) * unit], 0)

        for z in range(utts // 2):

            @pl.when(step == 2 + z)
            def _():
                value = (
                    dot_tn(second[...], act[...]) + dot_tn(send_far[:, : model // 2], act_far[...])
                ).astype(bf16)
                wide = value.shape[1] // 2
                for y in range(2):
                    for k in range(value.shape[0] // unit):
                        store_second(
                            2 * z + y,
                            value[k * unit : (k + 1) * unit, y * wide : (y + 1) * wide],
                            model // 2 + k * wide,
                        )

    if with_project:
        a_offset = low.shape[1] if with_feed else 0
        b_offset = b_keep.shape[3] - 640

        @pl.when(step == pl.num_programs(0) - 1)
        def _():
            total = [
                (gkv[i].astype(f32) + gkv_far[i].astype(f32)).astype(bf16) for i in range(2)
            ]
            near = jnp.concatenate([gq[...]] + total, 1)
            total = [
                (half_far[i + 1].astype(f32) + gkv_send[i].astype(f32)).astype(bf16) for i in range(2)
            ]
            far = jnp.concatenate([half_far[0]] + total, 1)
            value = (dot_tn(x[...], near[:, :512]) + dot_tn(x_far[...], far[:, :512])).astype(bf16)
            for side in range(2):

                @pl.when(where_ref[1] == side)
                def _():
                    store_first(a_keep, value[:, side * 256 : side * 256 + 256], a_offset)
                    store_first(a_send, value[:, 256 - side * 256 : 512 - side * 256], a_offset)

            value = (dot_tn(x[...], near[:, 512:]) + dot_tn(x_far[...], far[:, 512:])).astype(bf16)
            for u in range(utts):
                store_second(u, value[u * unit : (u + 1) * unit], b_offset)


def weight_grads(where, feed_part, project_part):
    in_specs, operands = [], []

    def fixed(shape, place=None):
        place = place or (lambda w: (0,) * len(shape))
        return pl.BlockSpec(shape, lambda i, w: place(w), pipeline_mode=pl.Buffered(1))

    if feed_part is not None:
        low, low_far, pre, pre_far, att, att_far, branch, act, act_far, second, send_far = feed_part
        rows, model = low.shape
        whole = fixed((rows, model))
        side = lambda i, w: jnp.where(i == 0, 1 - w[1], w[1])
        half = fixed((rows, model // 2), lambda w: (0, w[0]))
        chunk = pl.BlockSpec((rows, model), lambda i, w: (0, jnp.clip(i - 2, 0, 3)))
        in_specs += [
            whole,
            whole,
            pl.BlockSpec((rows, model), lambda i, w: (0, 2 * w[0] + side(i, w))),
            pl.BlockSpec((rows, model), lambda i, w: (0, side(i, w))),
            whole,
            whole,
            half,
            chunk,
            chunk,
            half,
            whole,
        ]
        operands += list(feed_part)
    if project_part is not None:
        x = project_part[0]
        rows, model = x.shape
        pair = fixed((2, rows, model // 2), lambda w: (0, 0, w[0]))
        in_specs += [
            fixed((rows, model)),
            fixed((rows, model)),
            fixed((rows, model // 2), lambda w: (0, w[0])),
            pair,
            pair,
            pair,
            fixed((3, rows, model // 2)),
        ]
        operands += list(project_part)
    a_width = (768 if feed_part is not None else 0) + (256 if project_part is not None else 0)
    b_width = (1920 if feed_part is not None else 0) + (640 if project_part is not None else 0)
    shapes = [(2, 2, 2, 96, a_width)] * 2 + [(2, 2, 96, b_width)] * 2
    steps = (6 if feed_part is not None else 0) + (1 if project_part is not None else 0)
    return pl.pallas_call(
        functools.partial(
            grads_kernel, with_feed=feed_part is not None, with_project=project_part is not None
        ),
        grid_spec=pltpu.PrefetchScalarGridSpec(
            num_scalar_prefetch=1,
            grid=(steps,),
            in_specs=in_specs,
            out_specs=[fixed(shape) for shape in shapes],
        ),
        out_shape=[jax.ShapeDtypeStruct(shape, bf16) for shape in shapes],
        compiler_params=pltpu.CompilerParams(vmem_limit_bytes=60 * MIB),
        name="weight_grads",
    )(where, *operands)


def finish_feed_kernel(core_ref, *refs):
    pieces, outs = refs[:4], refs[4:]
    grad_win, grad_wout, grad_wback = outs
    for layer in range(LAYERS):
        gap = 256 if layer == 0 else 0
        for side in range(2):
            piece = pieces[2 * layer + side]
            for parity in range(2):

                @pl.when(core_ref[0] == parity)
                def _():
                    core = parity if side == 0 else 1 - parity
                    at = core * 1536
                    grad_win[layer, :, at : at + 768] = piece[:, :768].astype(f32)
                    grad_win[layer, :, at + 768 : at + 1536] = piece[:, 768 + gap : 1536 + gap].astype(f32)
                    start = 1536 + 2 * gap
                    at = core * 384
                    grad_wout[layer, :, at : at + 384] = piece[:, start : start + 384].astype(f32)
                    start += 384
                    turned = jnp.concatenate(
                        [piece[:, start + 384 * k : start + 384 * k + 384] for k in range(4)], 0
                    )
                    grad_wback[layer, :, at : at + 384] = turned.astype(f32).T


def finish_project_kernel(core_ref, first, first_far, second, second_far, out):
    for layer, pieces in ((0, (first, first_far)), (1, (second, second_far))):
        for side in range(2):
            piece = pieces[side]
            for parity in range(2):

                @pl.when(core_ref[0] == parity)
                def _():
                    core = parity if side == 0 else 1 - parity
                    if layer == 0:
                        wide = piece[...]
                    else:
                        wide = jnp.concatenate(
                            [piece[:, 768:1024], piece[:, 1792:2048], piece[:, 3968:4608]], 1
                        )
                    for k in range(3):
                        at = 768 * k + 384 * core
                        out[layer, :, at : at + 384] = wide[:, 384 * k : 384 * k + 384].astype(f32)


def finish(kernel, core, pieces, shapes, name):
    memory = pl.BlockSpec(memory_space=pltpu.VMEM)
    return pl.pallas_call(
        kernel,
        in_specs=[pl.BlockSpec(memory_space=pltpu.SMEM)] + [memory] * len(pieces),
        out_specs=[memory] * len(shapes),
        out_shape=[jax.ShapeDtypeStruct(shape, f32) for shape in shapes],
        compiler_params=pltpu.CompilerParams(vmem_limit_bytes=48 * MIB),
        name=name,
    )(core, *pieces)


def pick(array, index):
    return lax.dynamic_index_in_dim(array, index, 0, keepdims=False)


def exchange(array, axis, bit, size):
    return lax.ppermute(array, axis, [(i, i ^ bit) for i in range(size)])


def chain(spots, group):
    x, y, z0, z1 = spots
    a_keep, a_send, b_keep, b_send = group
    a_far = exchange(a_send, "seq", 2, 4)
    b_far = exchange(b_send, "utt", 1, 8)

    def split(keep, far, spot):
        return (
            pick(keep, spot) + pick(far, spot),
            pick(keep, 1 - spot) + pick(far, 1 - spot),
        )

    a_keep, a_send = split(a_keep, a_far, y)
    b_keep, b_send = split(b_keep, b_far, z0)
    a_far = exchange(a_send, "utt", 1, 8)
    b_far = exchange(b_send, "utt", 2, 8)
    a_keep, a_send = split(a_keep, a_far, z0)
    b_keep, b_send = split(b_keep, b_far, z1)
    a_far = exchange(a_send, "utt", 2, 8)
    b_far = exchange(b_send, "utt", 4, 8)
    a_keep, a_send = split(a_keep, a_far, z1)
    b_keep = b_keep + b_far
    a_far = exchange(a_send, "utt", 4, 8)
    b_far = exchange(b_keep, "seq", 2, 4)
    a_keep = a_keep + a_far
    a_far = exchange(a_keep, "seq", 2, 4)
    left = jnp.where(x == 0, a_keep, a_far)
    right = jnp.where(x == 0, a_far, a_keep)
    near = jnp.concatenate([left, right, b_keep + b_far], 1)
    return near, exchange(near, "seq", 1, 4)


def body(sizes, frames, lengths, drop_bits, w_qkv, attn_bias, w_out, layer_bias, gains, w_in, in_bias, w_back, cotangent):
    seq_size, utt_size = sizes
    half = seq_size // 2
    utt_count, block_rows, model = frames.shape
    place = lax.axis_index("seq")
    utt_place = lax.axis_index("utt")
    mine = place // half
    swap = [(i, (i + half) % seq_size) for i in range(seq_size)]
    groups = [list(range(half)), list(range(half, seq_size))]
    by_chip = seq_size == 4 and utt_size == 8 and model == 768 and w_in.shape[2] == 3072

    def to_whole(array):
        far = lax.ppermute(pick(array, 1 - mine), "seq", swap)
        return jnp.concatenate([pick(array, mine), far], 0)

    def to_split(array):
        near, far = array[:block_rows], lax.ppermute(array[block_rows:], "seq", swap)
        first = jnp.where(mine == 0, near, far)
        second = jnp.where(mine == 0, far, near)
        return jnp.stack([first, second])

    def turn(array):
        return exchange(array, "seq", 1, seq_size) if by_chip else None

    core = (place % 2).astype(jnp.int32)
    where = jnp.stack([core, (place // 2).astype(jnp.int32), (utt_place % 2).astype(jnp.int32)])
    spots = (place // 2, utt_place % 2, utt_place // 2 % 2, utt_place // 4)
    core = core.reshape(1)
    length = pick(lengths, mine).reshape(1)
    live_bits = pick(drop_bits, mine)
    members = mine * half + jnp.arange(half, dtype=jnp.int32)
    if by_chip:
        members = jnp.stack([place, place ^ 1])
    base = jnp.stack([members, (members + half) % seq_size], 1).reshape(-1).astype(jnp.int32) * block_rows
    bias = jnp.concatenate([attn_bias[:, 0], jnp.zeros_like(attn_bias[:, 0]), attn_bias[:, 1]], 1)
    scale = jnp.concatenate([jnp.full((1, model), LOG2E * HEAD_DIM**-0.5, f32), jnp.ones((1, 2 * model), f32)], 1)

    x = low = to_whole(frames)
    saved_all = []
    for layer in range(LAYERS):
        live = live_bits[layer].reshape(1)
        kv = project(low, w_qkv, layer, bias[layer : layer + 1], scale, model, 2 * model)
        if by_chip:
            key_values = [kv, turn(kv)]
        else:
            key_values = [lax.all_gather(kv, "seq", axis=0, tiled=True, axis_index_groups=groups)]
        q = project(low, w_qkv, layer, bias[layer : layer + 1], scale, 0, model)
        att, extra = attend(length, base, q, key_values, block_rows)
        nxt, next_low, *saved = feed(live, x, att, layer, w_out, layer_bias, gains, w_in, in_bias, w_back)
        fars = (turn(low), turn(att), turn(saved[2]), turn(saved[3]))
        saved_all.append((low, q, key_values, att, extra, saved, live, fars))
        x, low = nxt, next_low
    mixed = to_split(low)

    grad = to_whole(cotangent)
    outputs = [None] * LAYERS
    smalls = [None] * LAYERS
    waiting = None
    sums = []
    for layer in reversed(range(LAYERS)):
        low, q, key_values, att, extra, saved, live, fars = saved_all[layer]
        sum_one, grad_att, pre, pre_send, second, branch, send, small, grad_ibias = feed_back(
            live, core, grad, saved, layer, w_out, gains, w_in, w_back
        )
        pre_far, send_far = turn(pre_send), turn(send)
        back = attend_back(length, base, core, q, grad_att, att, extra, key_values, block_rows)
        gq, bias_sums, gkv = back[:3]
        kind = f32 if layer > 0 else bf16
        smalls[layer] = jnp.concatenate([small[:6], bias_sums[:2], grad_ibias.reshape(4, model)], 0)
        if by_chip:
            gkv_send, half_send = back[3:]
            gkv_far, half_far = turn(gkv_send), turn(half_send)
            feed_part = (
                saved[2], fars[2], pre, pre_far, att, fars[1], branch, saved[3], fars[3], second, send_far
            )
            sums.append(chain(spots, weight_grads(where, feed_part, waiting)))
            waiting = (low, fars[0], gq, gkv, gkv_far, gkv_send, half_far)
            if layer == 0:
                sums.append(chain(spots, weight_grads(where, None, waiting)))
            grad = project_back(live, gq, gkv, gkv_far, grad, sum_one, w_qkv, layer, kind)
        else:
            gkv = lax.psum_scatter(gkv, "seq", scatter_dimension=1, tiled=True, axis_index_groups=groups)
            grad = project_back(live, gq, gkv, jnp.zeros_like(gkv), grad, sum_one, w_qkv, layer, kind)
            products = [
                dot_tn(low, jnp.concatenate([gq, gkv[0], gkv[1]], 1)),
                dot_tn(att, branch),
                dot_tn(saved[2], pre),
                dot_tn(saved[3], second),
            ]
            shares = [
                lax.psum_scatter(product.astype(bf16), "utt", scatter_dimension=0, tiled=True)
                for product in products
            ]
            outputs[layer] = [lax.psum(share, "seq").astype(f32) for share in shares]
    grad_frames = to_split(grad)
    small = lax.psum(jnp.stack(smalls), ("utt", "seq"))
    unit = model // utt_size
    mine_small = lax.dynamic_slice_in_dim(small[:, :8], utt_place * unit, unit, 2)
    ibias = small[:, 8:].reshape(LAYERS, 4 * model)
    ibias = lax.dynamic_slice_in_dim(ibias, 4 * utt_place * unit, 4 * unit, 1)
    if by_chip:
        (one, one_far), (two, two_far), (three, three_far) = sums
        grad_win, grad_wout, grad_wback = finish(
            finish_feed_kernel,
            core,
            (two, two_far, one, one_far),
            ((LAYERS, 96, 3072), (LAYERS, 96, 768), (LAYERS, 384, 768)),
            "finish_feed",
        )
        (grad_wqkv,) = finish(
            finish_project_kernel, core, (three, three_far, two, two_far), ((LAYERS, 96, 2304),), "finish_project"
        )
    else:
        grad_wqkv, grad_wout, grad_win, grad_wback = (
            jnp.stack([per[member] for per in outputs]) for member in range(4)
        )
    return (
        mixed,
        grad_frames,
        grad_wqkv,
        mine_small[:, 6:8],
        grad_wout,
        mine_small[:, 0:4],
        mine_small[:, 4:6],
        grad_win,
        ibias,
        grad_wback,
    )


def solution(mesh):
    frame_spec = P("utt", "seq", None)
    sizes = (mesh.shape["seq"], mesh.shape["utt"])
    return jax.shard_map(
        functools.partial(body, sizes),
        mesh=mesh,
        in_specs=(frame_spec, P("utt"), P("utt", None)) + (P(),) * 8 + (frame_spec,),
        out_specs=(
            frame_spec,
            frame_spec,
            P(None, "utt", None),
            P(None, None, "utt"),
            P(None, "utt", None),
            P(None, None, "utt"),
            P(None, None, "utt"),
            P(None, "utt", None),
            P(None, "utt"),
            P(None, "utt", None),
        ),
        check_vma=False,
    )
```

```python
import functools

import jax
import jax.numpy as jnp
from jax import lax
from jax.experimental import pallas as pl
from jax.experimental.pallas import tpu as pltpu
from jax.sharding import PartitionSpec as P

HEADS = 12
HEAD_DIM = 64
LAYERS = 2
LOG2E = 1.4426950408889634
LN2 = 0.6931471805599453
MASKED = -1e30
LANES = 128
MIB = 1 << 20

bf16 = jnp.bfloat16
f32 = jnp.float32


def dot(left, right):
    return jnp.dot(left, right, preferred_element_type=f32)


def dot_nt(left, right):
    return lax.dot_general(left, right, (((1,), (1,)), ((), ())), preferred_element_type=f32)


def dot_tn(left, right):
    return lax.dot_general(left, right, (((0,), (0,)), ((), ())), preferred_element_type=f32)


def call(kernel, ties, operands, in_specs, prefetch=0, grid=(), out_specs=(), scratch=(), cost=(0, 0), **options):
    count = prefetch + len(in_specs)
    ties = tuple(ties)

    def inner(*refs):
        kernel(*refs[:count], *refs[count + len(ties) :])

    return pl.pallas_call(
        inner,
        grid_spec=pltpu.PrefetchScalarGridSpec(
            num_scalar_prefetch=prefetch,
            grid=grid,
            in_specs=list(in_specs) + [pl.BlockSpec(memory_space=pl.ANY)] * len(ties),
            out_specs=out_specs,
            scratch_shapes=list(scratch),
        ),
        compiler_params=pltpu.CompilerParams(vmem_limit_bytes=60 * MIB),
        cost_estimate=pl.CostEstimate(flops=int(cost[0]), bytes_accessed=int(cost[1]), transcendentals=0),
        **options,
    )(*operands, *ties)


def whole_spec(shape, place=None):
    place = tuple(place) if place is not None else (0,) * len(shape)
    return pl.BlockSpec(shape, lambda *_: place, pipeline_mode=pl.Buffered(1))


def row_step(rows):
    for step in (256, 192, 128, 96, 64, 32, 16):
        if rows % step == 0:
            return step
    return rows


META_LENGTH, META_LIVE, META_CORE, META_X, META_Y, META_Z0, META_Z1, META_BASE = 0, 1, 3, 4, 5, 6, 7, 8


def project_kernel(meta_ref, x_ref, w_ref, bias_ref, out_ref, *, layer, first):
    del meta_ref
    part = dot(x_ref[...], w_ref[0])
    if first == 0:
        out_ref[...] = ((part + bias_ref[layer, 0:1]) * (LOG2E * HEAD_DIM**-0.5)).astype(bf16)
    else:
        keys = pl.program_id(0) < pl.num_programs(0) // 2
        shift = jnp.where(jnp.broadcast_to(keys, (1, part.shape[1])), 0.0, bias_ref[layer, 1:2])
        out_ref[...] = (part + shift).astype(bf16)


def project(meta, x, w_qkv, layer, bias, first, width, ties=(), block=384):
    rows, model = x.shape
    per = model // block
    return call(
        functools.partial(project_kernel, layer=layer, first=first),
        ties,
        (meta, x, w_qkv, bias),
        [
            whole_spec((rows, model)),
            pl.BlockSpec((1, model, block), lambda i, *_: (layer, 0, i + first // block)),
            pl.BlockSpec((LAYERS, 2, block), lambda i, *_: (0, 0, i % per)),
        ],
        prefetch=1,
        grid=(width // block,),
        out_specs=pl.BlockSpec((rows, block), lambda i, *_: (0, i)),
        out_shape=jax.ShapeDtypeStruct((rows, width), bf16),
        cost=(2 * rows * model * width * 2, 0),
        name="project",
    )


def lane_index():
    return lax.broadcasted_iota(jnp.int32, (1, LANES), 1)


def head_lanes(head):
    lane = lane_index()
    own = (lane < HEAD_DIM) if head == 0 else (lane >= HEAD_DIM)
    return jnp.where(own, 1.0, 0.0).astype(bf16), jnp.where(own, 0.0, 1.0).astype(bf16)


def fill_key_columns(meta_ref, columns_ref, block_rows):
    @pl.when(pl.program_id(0) == 0)
    def _():
        for block in range(columns_ref.shape[0] // block_rows):
            row = lax.broadcasted_iota(jnp.int32, (block_rows, LANES), 0) + meta_ref[META_BASE + block]
            slot = lax.broadcasted_iota(jnp.int32, (block_rows, LANES), 1) & (HEAD_DIM - 1)
            mask = jnp.where(row < meta_ref[META_LENGTH], 0.0, MASKED)
            column = jnp.where(slot == 3, mask, jnp.where(slot < 3, 1.0, 0.0))
            columns_ref[block * block_rows : (block + 1) * block_rows] = column.astype(bf16)


def split_parts(value, last):
    slot = lane_index() & (HEAD_DIM - 1)
    high = value.astype(bf16).astype(f32)
    rest = value - high
    middle = rest.astype(bf16).astype(f32)
    low = rest - middle
    tail = jnp.where(slot == 2, low, jnp.where(slot == 3, last, 0.0))
    return jnp.where(slot == 0, high, jnp.where(slot == 1, middle, tail)).astype(bf16)


def attend_kernel(meta_ref, q_ref, *refs, parts, block_rows, step):
    key_refs = refs[:parts]
    value_refs = refs[parts : 2 * parts]
    out_ref, extra_ref, columns_ref = refs[2 * parts :]
    rows = q_ref.shape[0]
    fill_key_columns(meta_ref, columns_ref, block_rows)
    lane = lane_index()
    slot = lane & (HEAD_DIM - 1)

    def operands(head):
        own, other = head_lanes(head)
        constant = jnp.where(slot == 3, 1.0, 0.0).astype(bf16) * other
        keys, values = [], []
        offset = 0
        for key_ref, value_ref in zip(key_refs, value_refs):
            size = key_ref.shape[0]
            keys.append(key_ref[...] * own + columns_ref[offset : offset + size] * other)
            values.append(value_ref[...] * own + other)
            offset += size
        return own, constant, keys, values

    def finish(start, size, sums, shifts):
        top = jnp.where(lane < HEAD_DIM, sums[0], sums[1])
        total = jnp.where(lane < HEAD_DIM, sums[1], sums[0])
        out_ref[pl.ds(start, size)] = (top / pltpu.roll(total, HEAD_DIM, 1)).astype(bf16)
        log_total = jnp.log2(total)
        if shifts is not None:
            log_total = log_total + jnp.where(lane < HEAD_DIM, shifts[1], shifts[0])
        extra_ref[pl.ds(start, size)] = split_parts(-log_total, 1.0)
        return total

    all_sums = []
    for head in range(2):
        own, constant, keys, values = operands(head)
        sums = []
        for start in range(0, rows, step):
            query = q_ref[start : start + step] * own + constant
            total = None
            for key, value in zip(keys, values):
                probs = jnp.exp2(dot_nt(query, key)).astype(bf16)
                term = dot(probs, value)
                total = term if total is None else total + term
            sums.append(total)
        all_sums.append(sums)
    bad = jnp.float32(0.0)
    for index, start in enumerate(range(0, rows, step)):
        total = finish(start, step, (all_sums[0][index], all_sums[1][index]), None)
        inside = (total > 2.0**-80) & (total < 2.0**100)
        bad = bad + jnp.sum(jnp.where(inside, 0.0, 1.0))

    @pl.when(bad > 0.0)
    def _():
        size = 16

        def body(index, carry):
            start = pl.multiple_of(index * size, size)
            sums, shifts = [], []
            for head in range(2):
                own, constant, keys, values = operands(head)
                query = q_ref[pl.ds(start, size)] * own + constant
                scores = [dot_nt(query, key) for key in keys]
                largest = functools.reduce(
                    jnp.maximum, [jnp.max(part, -1, keepdims=True) for part in scores]
                )
                total = None
                for part, value in zip(scores, values):
                    term = dot(jnp.exp2(part - largest).astype(bf16), value)
                    total = term if total is None else total + term
                sums.append(total)
                shifts.append(largest)
            finish(start, size, sums, shifts)
            return carry

        lax.fori_loop(0, rows // size, body, 0)


def attend(meta, q, key_values, block_rows, ties=()):
    rows, model = q.shape
    pairs = model // LANES
    parts = len(key_values)
    total = sum(part.shape[0] for part in key_values)

    def column(size, shift=0):
        return pl.BlockSpec((size, LANES), lambda i, *_: (0, i + shift))

    return call(
        functools.partial(attend_kernel, parts=parts, block_rows=block_rows, step=row_step(rows)),
        ties,
        (meta, q, *key_values, *key_values),
        [column(rows)]
        + [column(part.shape[0]) for part in key_values]
        + [column(part.shape[0], pairs) for part in key_values],
        prefetch=1,
        grid=(pairs,),
        out_specs=[column(rows), column(rows)],
        out_shape=[jax.ShapeDtypeStruct((rows, model), bf16)] * 2,
        scratch=[pltpu.VMEM((total, LANES), bf16)],
        cost=(16 * rows * total * model, 0),
        name="attend",
    )


def attend_back_kernel(
    meta_ref, q_ref, grad_ref, out_ref, extra_ref, *refs, parts, block_rows, step
):
    key_refs = refs[:parts]
    value_refs = refs[parts : 2 * parts]
    grad_query_ref, bias_ref = refs[2 * parts : 2 * parts + 2]
    grad_refs = refs[2 * parts + 2 : 3 * parts + 2]
    half_ref = refs[3 * parts + 2] if parts == 2 else None
    columns_ref = refs[-1]
    rows = q_ref.shape[0]
    fill_key_columns(meta_ref, columns_ref, block_rows)
    lane = lane_index()
    slot = lane & (HEAD_DIM - 1)
    value_column = jnp.where(slot < 3, 1.0, 0.0).astype(bf16)
    from_lane = lax.broadcasted_iota(jnp.int32, (LANES, LANES), 0)
    to_lane = lax.broadcasted_iota(jnp.int32, (LANES, LANES), 1)
    swap = jnp.where((from_lane < HEAD_DIM) != (to_lane < HEAD_DIM), -1.0, 0.0).astype(bf16)
    grad_keys = [None] * parts
    grad_values = [None] * parts
    heads = [head_lanes(head) for head in range(2)]
    offsets = []
    offset = 0
    for part in range(parts):
        offsets.append(offset)
        offset += key_refs[part].shape[0]

    def add(old, new):
        return new if old is None else old + new

    query_sum = None
    for start in range(0, rows, step):
        query, grad = q_ref[start : start + step], grad_ref[start : start + step]
        extra = extra_ref[start : start + step]
        product = grad.astype(f32) * out_ref[start : start + step].astype(f32)
        high = product.astype(bf16)
        low = (product - high.astype(f32)).astype(bf16)
        inner = split_parts(dot(high, swap) + dot(low, swap), 0.0)
        grad_query = None
        for head in range(2):
            own, other = heads[head]
            query_own, grad_own = query * own, grad * own
            query_full, grad_full = query_own + extra * other, grad_own + inner * other
            query_turned, grad_turned = query_own.T, grad_own.T
            for part in range(parts):
                size = key_refs[part].shape[0]
                key_own = key_refs[part][...] * own
                key_full = key_own + columns_ref[offsets[part] : offsets[part] + size] * other
                value_full = value_refs[part][...] * own + value_column * other
                probs = jnp.exp2(dot_nt(query_full, key_full))
                grad_scores = (probs * dot_nt(grad_full, value_full)).astype(bf16)
                grad_values[part] = add(grad_values[part], dot(grad_turned, probs.astype(bf16)))
                grad_keys[part] = add(grad_keys[part], dot(query_turned, grad_scores))
                grad_query = add(grad_query, dot(grad_scores, key_own))
        grad_query = grad_query * HEAD_DIM**-0.5
        query_sum = add(query_sum, column_sum(grad_query))
        grad_query_ref[start : start + step] = grad_query.astype(bf16)
    value_sum = None
    for part in range(parts):
        grad_value = grad_values[part].T
        value_sum = add(value_sum, column_sum(grad_value))
        grad_refs[part][0] = (grad_keys[part] * LN2).T.astype(bf16)
        grad_refs[part][1] = grad_value.astype(bf16)
    bias_ref[0:1] = query_sum
    bias_ref[1:2] = value_sum
    bias_ref[2:8] = jnp.zeros((6, LANES), f32)
    if half_ref is not None:
        first = (1 - meta_ref[META_CORE]) * (pl.num_programs(0) // 2)
        index = pl.program_id(0)

        @pl.when((index >= first) & (index < first + pl.num_programs(0) // 2))
        def _():
            half_ref[0] = grad_query_ref[...]
            half_ref[1] = grad_refs[0][0]
            half_ref[2] = grad_refs[0][1]


def attend_back(meta, q, grad, out, extra, key_values, block_rows, ties=()):
    rows, model = q.shape
    pairs = model // LANES
    parts = len(key_values)
    sizes = [part.shape[0] for part in key_values]

    def column(size, shift=0):
        return pl.BlockSpec((size, LANES), lambda i, *_: (0, i + shift))

    def stack(count, size):
        return pl.BlockSpec((count, size, LANES), lambda i, *_: (0, 0, i))

    def half_place(i, meta):
        return 0, 0, jnp.clip(i - (1 - meta[META_CORE]) * (pairs // 2), 0, pairs // 2 - 1)

    out_specs = [column(rows), pl.BlockSpec((8, LANES), lambda i, *_: (0, i))]
    out_specs += [stack(2, size) for size in sizes]
    out_shape = [jax.ShapeDtypeStruct((rows, model), bf16), jax.ShapeDtypeStruct((8, model), f32)]
    out_shape += [jax.ShapeDtypeStruct((2, size, model), bf16) for size in sizes]
    if parts == 2:
        out_specs.append(pl.BlockSpec((3, rows, LANES), half_place))
        out_shape.append(jax.ShapeDtypeStruct((3, rows, model // 2), bf16))
    return call(
        functools.partial(attend_back_kernel, parts=parts, block_rows=block_rows, step=row_step(rows)),
        ties,
        (meta, q, grad, out, extra, *key_values, *key_values),
        [column(rows)] * 4 + [column(size) for size in sizes] + [column(size, pairs) for size in sizes],
        prefetch=1,
        grid=(pairs,),
        out_specs=out_specs,
        scratch=[pltpu.VMEM((sum(sizes), LANES), bf16)],
        out_shape=out_shape,
        cost=(32 * rows * sum(sizes) * model, 0),
        name="attend_back",
    )


def norm_parts(value):
    mean = jnp.mean(value, -1, keepdims=True)
    centred = value - mean
    inverse = lax.rsqrt(jnp.mean(centred * centred, -1, keepdims=True) + 1e-05)
    return centred * inverse, inverse


def gelu_parts(pre):
    size = jnp.abs(pre)
    ratio = 1.0 / (1.0 + size * (0.3275911 * 0.7071067811865476))
    poly = 1.061405429 * ratio - 1.453152027
    poly = poly * ratio + 1.421413741
    poly = poly * ratio - 0.284496736
    poly = (poly * ratio + 0.254829592) * ratio
    bell = jnp.exp2(pre * pre * (-0.5 * LOG2E))
    tail = 0.5 * poly * bell
    share = jnp.where(pre < 0.0, tail, 1.0 - tail)
    return pre * share, share + pre * bell * 0.3989422804014327


def feed_kernel(
    meta_ref, x_ref, att_ref, wout_ref, lbias_ref, gains_ref, win_ref, ibias_ref, wback_ref,
    next_ref, next_low_ref, norm_one_ref, inv_one_ref, low_ref, act_ref, slope_ref, norm_two_ref, inv_two_ref,
    full_ref, acc_ref, *, step, layer,
):
    rows = x_ref.shape[0]
    index = pl.program_id(0)

    @pl.when(index == 0)
    def _():
        for start in range(0, rows, step):
            here = slice(start, start + step)
            total = (
                x_ref[here].astype(f32) + dot(att_ref[here], wout_ref[0]) + lbias_ref[0, 0:1]
            )
            normed, inverse = norm_parts(total)
            full = normed * gains_ref[0, 0:1] + lbias_ref[0, 1:2]
            norm_one_ref[here] = normed.astype(bf16)
            inv_one_ref[here] = jnp.broadcast_to(inverse, (step, LANES))
            low_ref[here] = full.astype(bf16)
            full_ref[here] = full + lbias_ref[0, 2:3]
            acc_ref[here] = jnp.zeros((step, x_ref.shape[1]), f32)

    for start in range(0, rows, step):
        here = slice(start, start + step)
        pre = dot(low_ref[here], win_ref[0]) + ibias_ref[layer : layer + 1]
        active, slope = gelu_parts(pre)
        active = active.astype(bf16)
        act_ref[here] = active
        slope_ref[here] = slope.astype(bf16)
        acc_ref[here] += dot(active, wback_ref[0])

    @pl.when(index == pl.num_programs(0) - 1)
    def _():
        for start in range(0, rows, step):
            here = slice(start, start + step)
            normed, inverse = norm_parts(full_ref[here] + acc_ref[here])
            norm_two_ref[here] = normed.astype(bf16)
            inv_two_ref[here] = jnp.broadcast_to(inverse, (step, LANES))
            result = normed * gains_ref[0, 1:2] + lbias_ref[0, 3:4]
            live = jnp.broadcast_to(meta_ref[META_LIVE + layer], result.shape) > 0
            result = jnp.where(live, result, x_ref[here].astype(f32))
            next_ref[here] = result
            next_low_ref[here] = result.astype(bf16)


def feed(meta, x, att, layer, w_out, layer_bias, gains, w_in, in_bias, w_back, ties=(), block=512):
    rows, model = x.shape
    hidden = w_in.shape[2]
    whole = whole_spec((rows, model))
    lanes = whole_spec((rows, LANES))
    chunk = pl.BlockSpec((rows, block), lambda i, *_: (0, i))
    return call(
        functools.partial(feed_kernel, step=row_step(rows), layer=layer),
        ties,
        (meta, x, att, w_out, layer_bias, gains, w_in, in_bias, w_back),
        [
            whole,
            whole,
            whole_spec((1, model, model), (layer, 0, 0)),
            whole_spec((1, 4, model), (layer, 0, 0)),
            whole_spec((1, 2, model), (layer, 0, 0)),
            pl.BlockSpec((1, model, block), lambda i, *_: (layer, 0, i)),
            pl.BlockSpec((LAYERS, block), lambda i, *_: (0, i)),
            pl.BlockSpec((1, block, model), lambda i, *_: (layer, i, 0)),
        ],
        prefetch=1,
        grid=(hidden // block,),
        out_specs=[whole, whole, whole, lanes, whole, chunk, chunk, whole, lanes],
        out_shape=[
            jax.ShapeDtypeStruct((rows, model), f32),
            jax.ShapeDtypeStruct((rows, model), bf16),
            jax.ShapeDtypeStruct((rows, model), bf16),
            jax.ShapeDtypeStruct((rows, LANES), f32),
            jax.ShapeDtypeStruct((rows, model), bf16),
            jax.ShapeDtypeStruct((rows, hidden), bf16),
            jax.ShapeDtypeStruct((rows, hidden), bf16),
            jax.ShapeDtypeStruct((rows, model), bf16),
            jax.ShapeDtypeStruct((rows, LANES), f32),
        ],
        scratch=[pltpu.VMEM((rows, model), f32)] * 2,
        cost=(2 * rows * model * (2 * hidden + model) * 2, 0),
        name="feed",
    )


def norm_back(normed, inverse, grad, gain):
    grad_normed = grad * gain
    mean = jnp.mean(grad_normed, -1, keepdims=True)
    mean_product = jnp.mean(grad_normed * normed, -1, keepdims=True)
    return inverse * (grad_normed - mean - normed * mean_product)


def column_sum(value):
    return jnp.sum(value, 0, keepdims=True)


def feed_back_kernel(
    meta_ref, grad_ref, norm_two_ref, inv_two_ref, gains_ref, slope_ref, win_ref, wback_ref,
    norm_one_ref, inv_one_ref, wout_ref,
    sum_one_ref, grad_att_ref, pre_ref, pre_send_ref, second_low_ref, branch_ref, send_ref, small_ref, grad_ibias_ref,
    second_ref, acc_ref, *, step, layer,
):
    rows, model = grad_ref.shape
    index = pl.program_id(0)
    count = pl.num_programs(0)
    starts = range(0, rows, step)
    far = pl.multiple_of((1 - meta_ref[META_CORE]) * (model // 2), LANES)

    def add(old, new):
        return new if old is None else old + new

    @pl.when(index == 0)
    def _():
        gain_sum = shift_sum = bias_sum = None
        for start in starts:
            here = slice(start, start + step)
            grad = grad_ref[here].astype(f32)
            through = jnp.where(jnp.broadcast_to(meta_ref[META_LIVE + layer], grad.shape) > 0, grad, 0.0)
            normed = norm_two_ref[here].astype(f32)
            back = norm_back(normed, inv_two_ref[here, 0:1], through, gains_ref[0, 1:2])
            second_ref[here] = back
            second_low_ref[here] = back.astype(bf16)
            acc_ref[here] = jnp.zeros(back.shape, f32)
            gain_sum = add(gain_sum, column_sum(through * normed))
            shift_sum = add(shift_sum, column_sum(through))
            bias_sum = add(bias_sum, column_sum(back))
        small_ref[3:4] = shift_sum
        small_ref[2:3] = bias_sum
        small_ref[5:6] = gain_sum
        small_ref[6:8] = jnp.zeros((2, model), f32)
        send_ref[:, : model // 2] = second_low_ref[:, pl.ds(far, model // 2)]

    bias_total = None
    for start in starts:
        here = slice(start, start + step)
        grad_pre = dot_nt(second_low_ref[here], wback_ref[0]) * slope_ref[here].astype(f32)
        bias_total = add(bias_total, column_sum(grad_pre))
        pre_low = grad_pre.astype(bf16)
        pre_ref[here] = pre_low
        acc_ref[here] += dot_nt(pre_low, win_ref[0])
    grad_ibias_ref[...] = bias_total
    first = (1 - meta_ref[META_CORE]) * (count // 2)

    @pl.when((index >= first) & (index < first + count // 2))
    def _():
        pre_send_ref[...] = pre_ref[...]

    @pl.when(index == count - 1)
    def _():
        gain_sum = shift_sum = bias_sum = None
        for start in starts:
            here = slice(start, start + step)
            grad_first = second_ref[here] + acc_ref[here]
            normed = norm_one_ref[here].astype(f32)
            back = norm_back(normed, inv_one_ref[here, 0:1], grad_first, gains_ref[0, 0:1])
            sum_one_ref[here] = back
            branch = back.astype(bf16)
            branch_ref[here] = branch
            grad_att_ref[here] = dot_nt(branch, wout_ref[0]).astype(bf16)
            gain_sum = add(gain_sum, column_sum(grad_first * normed))
            shift_sum = add(shift_sum, column_sum(grad_first))
            bias_sum = add(bias_sum, column_sum(back))
        small_ref[1:2] = shift_sum
        small_ref[0:1] = bias_sum
        small_ref[4:5] = gain_sum
        send_ref[:, model // 2 :] = branch_ref[:, pl.ds(far, model // 2)]


def feed_back(meta, grad, saved, layer, w_out, gains, w_in, w_back, ties=(), block=512):
    norm_one, inv_one, low, act, slope, norm_two, inv_two = saved
    rows, model = grad.shape
    hidden = w_in.shape[2]
    count = hidden // block
    whole = whole_spec((rows, model))
    lanes = whole_spec((rows, LANES))
    chunk = pl.BlockSpec((rows, block), lambda i, *_: (0, i))

    def half_place(i, meta):
        return 0, jnp.clip(i - (1 - meta[META_CORE]) * (count // 2), 0, count // 2 - 1)

    return call(
        functools.partial(feed_back_kernel, step=row_step(rows), layer=layer),
        ties,
        (meta, grad, norm_two, inv_two, gains, slope, w_in, w_back, norm_one, inv_one, w_out),
        [
            whole,
            whole,
            lanes,
            whole_spec((1, 2, model), (layer, 0, 0)),
            chunk,
            pl.BlockSpec((1, model, block), lambda i, *_: (layer, 0, i)),
            pl.BlockSpec((1, block, model), lambda i, *_: (layer, i, 0)),
            whole,
            lanes,
            whole_spec((1, model, model), (layer, 0, 0)),
        ],
        prefetch=1,
        grid=(count,),
        out_specs=[
            whole,
            whole,
            chunk,
            pl.BlockSpec((rows, block), half_place),
            whole,
            whole,
            whole,
            whole_spec((8, model)),
            pl.BlockSpec((1, block), lambda i, *_: (0, i)),
        ],
        scratch=[pltpu.VMEM((rows, model), f32)] * 2,
        out_shape=[
            jax.ShapeDtypeStruct((rows, model), f32),
            jax.ShapeDtypeStruct((rows, model), bf16),
            jax.ShapeDtypeStruct((rows, hidden), bf16),
            jax.ShapeDtypeStruct((rows, hidden // 2), bf16),
            jax.ShapeDtypeStruct((rows, model), bf16),
            jax.ShapeDtypeStruct((rows, model), bf16),
            jax.ShapeDtypeStruct((rows, model), bf16),
            jax.ShapeDtypeStruct((8, model), f32),
            jax.ShapeDtypeStruct((1, hidden), f32),
        ],
        cost=(2 * rows * model * (2 * hidden + model) * 2, 0),
        name="feed_back",
    )


def project_back_kernel(meta_ref, gq_ref, gkv_ref, far_ref, grad_ref, sum_one_ref, w_ref, out_ref, acc_ref, *, step, layer):
    index = pl.program_id(0)
    rows = gq_ref.shape[0]

    @pl.when(index == 0)
    def _():
        for start in range(0, rows, step):
            here = slice(start, start + step)
            grad = grad_ref[here].astype(f32)
            live = jnp.broadcast_to(meta_ref[META_LIVE + layer], grad.shape) > 0
            skipped = jnp.where(live, 0.0, grad)
            acc_ref[here] = skipped + sum_one_ref[here] + dot_nt(gq_ref[here], w_ref[0])

    @pl.when(index == 1)
    def _():
        for start in range(0, rows, step):
            here = slice(start, start + step)
            total = (gkv_ref[0, here].astype(f32) + far_ref[0, here].astype(f32)).astype(bf16)
            acc_ref[here] += dot_nt(total, w_ref[0])

    @pl.when(index == 2)
    def _():
        for start in range(0, rows, step):
            here = slice(start, start + step)
            total = (gkv_ref[0, here].astype(f32) + far_ref[0, here].astype(f32)).astype(bf16)
            out_ref[here] = (acc_ref[here] + dot_nt(total, w_ref[0])).astype(out_ref.dtype)


def project_back(meta, gq, gkv, far, grad, sum_one, w_qkv, layer, kind, ties=()):
    rows, model = gq.shape
    whole = whole_spec((rows, model))
    part = pl.BlockSpec((1, rows, model), lambda i, *_: (jnp.maximum(i - 1, 0), 0, 0))
    return call(
        functools.partial(project_back_kernel, step=row_step(rows), layer=layer),
        ties,
        (meta, gq, gkv, far, grad, sum_one, w_qkv),
        [
            whole,
            part,
            part,
            whole,
            whole,
            pl.BlockSpec((1, model, model), lambda i, *_: (layer, 0, i)),
        ],
        prefetch=1,
        grid=(3,),
        out_specs=whole,
        out_shape=jax.ShapeDtypeStruct((rows, model), kind),
        scratch=[pltpu.VMEM((rows, model), f32)],
        cost=(2 * rows * model * 3 * model * 2, 0),
        name="project_back",
    )


def small_columns(refs):
    rows = []
    for layer in range(LAYERS):
        small, bias_sums = refs[3 * layer], refs[3 * layer + 1]
        rows += [small[0:6], bias_sums[0:2], jnp.zeros((8, small.shape[1]), f32)]
    model = rows[0].shape[1]
    rows.append(jnp.zeros((LANES - 16 * LAYERS, model), f32))
    columns = jnp.concatenate(rows, 0).T
    lane = lane_index()
    for layer in range(LAYERS):
        hidden = refs[3 * layer + 2][...]
        turned = jnp.concatenate([hidden, jnp.zeros((LANES - 1, hidden.shape[1]), f32)], 0).T[:, 0:1]
        for k in range(4):
            piece = jnp.concatenate(
                [turned[384 * u + 96 * k : 384 * u + 96 * k + 96] for u in range(8)], 0
            )
            columns = jnp.where(lane == 16 * layer + 8 + k, piece, columns)
    return columns.astype(bf16)


def grads_kernel(meta_ref, *refs, with_feed, with_project, with_small):
    refs = list(refs)
    if with_feed:
        low, low_far, pre, pre_far, att, att_far, branch, act, act_far, second, send_far = refs[:11]
        del refs[:11]
    if with_project:
        x, x_far, gq, gkv, gkv_far, gkv_send, half_far = refs[:7]
        del refs[:7]
    if with_small:
        small_refs = refs[:6]
        del refs[:6]
    a_keep, a_send, b_keep, b_send = refs[:4]
    step = pl.program_id(0)
    unit = a_keep.shape[3]
    utts = 8

    def store_first(ref, value, offset):
        for u in range(utts):
            ref[u % 2, u // 2 % 2, u // 4, :, offset : offset + value.shape[1]] = value[u * unit : (u + 1) * unit]

    def store_second(pieces):
        for parity in range(2):

            @pl.when(meta_ref[META_Y] == parity)
            def _():
                for u, value, offset in pieces:
                    ref = b_keep if u % 2 == parity else b_send
                    ref[u // 2 % 2, u // 4, :, offset : offset + value.shape[1]] = value

    def rows_of(value, offset):
        return [(u, value[u * unit : (u + 1) * unit], offset) for u in range(utts)]

    if with_feed:
        model = low.shape[1]

        @pl.when(step <= 1)
        def _():
            value = (dot_tn(low[...], pre[...]) + dot_tn(low_far[...], pre_far[...])).astype(bf16)

            @pl.when(step == 0)
            def _():
                store_first(a_send, value, 0)

            @pl.when(step == 1)
            def _():
                store_first(a_keep, value, 0)

        @pl.when(step == 1)
        def _():
            value = (
                dot_tn(att[...], branch[...]) + dot_tn(att_far[...], send_far[:, model // 2 :])
            ).astype(bf16)
            store_second(rows_of(value, 0))

        for z in range(utts // 2):

            @pl.when(step == 2 + z)
            def _():
                value = (
                    dot_tn(second[...], act[...]) + dot_tn(send_far[:, : model // 2], act_far[...])
                ).astype(bf16)
                wide = value.shape[1] // 2
                store_second(
                    [
                        (
                            2 * z + y,
                            value[k * unit : (k + 1) * unit, y * wide : (y + 1) * wide],
                            model // 2 + k * wide,
                        )
                        for y in range(2)
                        for k in range(value.shape[0] // unit)
                    ]
                )

    if with_project:
        a_offset = low.shape[1] if with_feed else 0
        b_offset = 1920 if with_feed else 0

        @pl.when(step == pl.num_programs(0) - 1)
        def _():
            total = [
                (gkv[i].astype(f32) + gkv_far[i].astype(f32)).astype(bf16) for i in range(2)
            ]
            near = jnp.concatenate([gq[...], total[0]], 1)
            far_total = [
                (half_far[i + 1].astype(f32) + gkv_send[i].astype(f32)).astype(bf16) for i in range(2)
            ]
            far = jnp.concatenate([half_far[0], far_total[0]], 1)
            value = (dot_tn(x[...], near) + dot_tn(x_far[...], far)).astype(bf16)
            for side in range(2):

                @pl.when(meta_ref[META_X] == side)
                def _():
                    store_first(a_keep, value[:, side * 384 : side * 384 + 384], a_offset)
                    store_first(a_send, value[:, 384 - side * 384 : 768 - side * 384], a_offset)

            value = (dot_tn(x[...], total[1]) + dot_tn(x_far[...], far_total[1])).astype(bf16)
            store_second(rows_of(value, b_offset))
            if with_small:
                store_second(rows_of(small_columns(small_refs), b_offset + 384))


def weight_grads(meta, feed_part, project_part, small_part, ties=()):
    in_specs, operands = [], [meta]
    flops = 0

    def half_spec(shape):
        count = len(shape) - 1
        return pl.BlockSpec(
            shape, lambda i, m: (0,) * count + (m[META_CORE],), pipeline_mode=pl.Buffered(1)
        )

    if feed_part is not None:
        rows, model = feed_part[0].shape
        whole = whole_spec((rows, model))
        half = half_spec((rows, model // 2))
        chunk = pl.BlockSpec((rows, model), lambda i, *_: (0, jnp.clip(i - 2, 0, 3)))

        def side(i, m):
            return jnp.where(i == 0, 1 - m[META_X], m[META_X])

        in_specs += [
            whole,
            whole,
            pl.BlockSpec((rows, model), lambda i, m: (0, 2 * m[META_CORE] + side(i, m))),
            pl.BlockSpec((rows, model), lambda i, m: (0, side(i, m))),
            whole,
            whole,
            half,
            chunk,
            chunk,
            half,
            whole,
        ]
        operands += list(feed_part)
        flops += 2 * rows * model * 9 * model
    if project_part is not None:
        rows, model = project_part[0].shape
        pair = half_spec((2, rows, model // 2))
        in_specs += [
            whole_spec((rows, model)),
            whole_spec((rows, model)),
            half_spec((rows, model // 2)),
            pair,
            pair,
            pair,
            whole_spec((3, rows, model // 2)),
        ]
        operands += list(project_part)
        flops += 2 * rows * model * 3 * model
    if small_part is not None:
        in_specs += [whole_spec(part.shape) for part in small_part]
        operands += list(small_part)
    a_width = (768 if feed_part is not None else 0) + (384 if project_part is not None else 0)
    b_width = (1920 if feed_part is not None else 0) + (384 if project_part is not None else 0)
    b_width += LANES if small_part is not None else 0
    shapes = [(2, 2, 2, 96, a_width)] * 2 + [(2, 2, 96, b_width)] * 2
    steps = (6 if feed_part is not None else 0) + (1 if project_part is not None else 0)
    return call(
        functools.partial(
            grads_kernel,
            with_feed=feed_part is not None,
            with_project=project_part is not None,
            with_small=small_part is not None,
        ),
        ties,
        operands,
        in_specs,
        prefetch=1,
        grid=(steps,),
        out_specs=[whole_spec(shape) for shape in shapes],
        out_shape=[jax.ShapeDtypeStruct(shape, bf16) for shape in shapes],
        cost=(2 * flops, 0),
        name="weight_grads",
    )


def combine_kernel(meta_ref, *refs, spots):
    count = len(spots)
    for index, spot in enumerate(spots):
        keep, far = refs[2 * index], refs[2 * index + 1]
        outs = refs[2 * count :]
        if spot is None:
            outs[2 * index][...] = keep[...] + far[...]
            outs[2 * index + 1][...] = jnp.zeros(outs[2 * index + 1].shape, bf16)
        else:
            at = meta_ref[spot]
            outs[2 * index][...] = keep[at] + far[at]
            outs[2 * index + 1][...] = keep[1 - at] + far[1 - at]


def combine(meta, arrays, spots, ties=()):
    operands, in_specs, shapes = [meta], [], []
    for (keep, far), spot in zip(arrays, spots):
        operands += [keep, far]
        in_specs += [whole_spec(keep.shape)] * 2
        shapes += [keep.shape, (16, LANES)] if spot is None else [keep.shape[1:]] * 2
    return call(
        functools.partial(combine_kernel, spots=spots),
        ties,
        operands,
        in_specs,
        prefetch=1,
        grid=(1,),
        out_specs=[whole_spec(shape) for shape in shapes],
        out_shape=[jax.ShapeDtypeStruct(shape, bf16) for shape in shapes],
        cost=(0, 4 * sum(keep.size for keep, _ in arrays)),
        name="combine",
    )


def join_kernel(meta_ref, a_keep, a_far, b_keep, b_far, out_ref):
    width = a_keep.shape[1]
    for side in range(2):

        @pl.when(meta_ref[META_X] == side)
        def _():
            out_ref[:, side * width : (side + 1) * width] = a_keep[...]
            out_ref[:, (1 - side) * width : (2 - side) * width] = a_far[...]

    out_ref[:, 2 * width :] = b_keep[...] + b_far[...]


def join(meta, a_keep, a_far, b_keep, b_far, ties=()):
    rows, width = a_keep.shape
    total = 2 * width + b_keep.shape[1]
    return call(
        join_kernel,
        ties,
        (meta, a_keep, a_far, b_keep, b_far),
        [whole_spec(part.shape) for part in (a_keep, a_far, b_keep, b_far)],
        prefetch=1,
        grid=(1,),
        out_specs=whole_spec((rows, total)),
        out_shape=jax.ShapeDtypeStruct((rows, total), bf16),
        name="join",
    )


def finish_feed_kernel(meta_ref, zero, zero_far, one, one_far, grad_win, grad_wout, grad_wback):
    pieces = ((zero, zero_far), (one, one_far))
    for layer in range(LAYERS):
        gap = 384 if layer == 0 else 0
        for side in range(2):
            piece = pieces[layer][side]
            for parity in range(2):

                @pl.when(meta_ref[META_CORE] == parity)
                def _():
                    core = parity if side == 0 else 1 - parity
                    at = core * 1536
                    grad_win[layer, :, at : at + 768] = piece[:, :768].astype(f32)
                    grad_win[layer, :, at + 768 : at + 1536] = piece[:, 768 + gap : 1536 + gap].astype(f32)
                    start = 1536 + 2 * gap
                    at = core * 384
                    grad_wout[layer, :, at : at + 384] = piece[:, start : start + 384].astype(f32)
                    start += 384
                    turned = jnp.concatenate(
                        [piece[:, start + 384 * k : start + 384 * k + 384] for k in range(4)], 0
                    )
                    grad_wback[layer, :, at : at + 384] = turned.astype(f32).T


def finish_project_kernel(
    meta_ref, zero, zero_far, one, one_far, out, attn_bias, layer_bias, gains, in_bias
):
    pieces = ((zero, zero_far), (one, one_far))
    for layer in range(LAYERS):
        for side in range(2):
            piece = pieces[layer][side]
            places = (0, 384, 768) if layer == 0 else (768, 1920, 4224)
            for parity in range(2):

                @pl.when(meta_ref[META_CORE] == parity)
                def _():
                    core = parity if side == 0 else 1 - parity
                    for k in range(3):
                        at = 768 * k + 384 * core
                        out[layer, :, at : at + 384] = piece[:, places[k] : places[k] + 384].astype(f32)

    small = zero[:, 1152:].astype(f32) + zero_far[:, 1152:].astype(f32)
    small = jnp.concatenate([small, jnp.zeros((LANES - small.shape[0], LANES), f32)], 0).T
    for layer in range(LAYERS):
        row = 16 * layer
        unit = zero.shape[0]
        layer_bias[layer] = small[row : row + 4, :unit]
        gains[layer] = small[row + 4 : row + 6, :unit]
        attn_bias[layer] = small[row + 6 : row + 8, :unit]
        in_bias[layer] = small[row + 8 : row + 12, :unit]


def finish(kernel, meta, pieces, shapes, name, ties=()):
    return call(
        kernel,
        ties,
        (meta, *pieces),
        [whole_spec(piece.shape) for piece in pieces],
        prefetch=1,
        grid=(1,),
        out_specs=[whole_spec(shape) for shape in shapes],
        out_shape=[jax.ShapeDtypeStruct(shape, f32) for shape in shapes],
        name=name,
    )


def pick(array, index):
    return lax.dynamic_index_in_dim(array, index, 0, keepdims=False)


def exchange(array, axis, bit, size):
    return lax.ppermute(array, axis, [(i, i ^ bit) for i in range(size)])


def chain_steps(meta, group):
    a_keep, a_send, b_keep, b_send = group
    a_far, b_far = exchange(a_send, "seq", 2, 4), exchange(b_send, "utt", 1, 8)
    ties = yield (a_keep,)
    a_keep, a_send, b_keep, b_send = combine(
        meta, ((a_keep, a_far), (b_keep, b_far)), (META_Y, META_Z0), ties
    )
    a_far, b_far = exchange(a_send, "utt", 1, 8), exchange(b_send, "utt", 2, 8)
    ties = yield (a_keep,)
    a_keep, a_send, b_keep, b_send = combine(
        meta, ((a_keep, a_far), (b_keep, b_far)), (META_Z0, META_Z1), ties
    )
    a_far, b_far = exchange(a_send, "utt", 2, 8), exchange(b_send, "utt", 4, 8)
    ties = yield (a_keep,)
    a_keep, a_send, b_keep, _ = combine(
        meta, ((a_keep, a_far), (b_keep, b_far)), (META_Z1, None), ties
    )
    a_far, b_far = exchange(a_send, "utt", 4, 8), exchange(b_keep, "seq", 2, 4)
    ties = yield (a_keep,)
    a_keep, _ = combine(meta, ((a_keep, a_far),), (None,), ties)
    a_far = exchange(a_keep, "seq", 2, 4)
    ties = yield (a_keep,)
    near = join(meta, a_keep, a_far, b_keep, b_far, ties)
    yield (near,), (near, exchange(near, "seq", 1, 4))


def body(sizes, frames, lengths, drop_bits, w_qkv, attn_bias, w_out, layer_bias, gains, w_in, in_bias, w_back, cotangent):
    seq_size, utt_size = sizes
    half = seq_size // 2
    utt_count, block_rows, model = frames.shape
    place = lax.axis_index("seq").astype(jnp.int32)
    utt_place = lax.axis_index("utt").astype(jnp.int32)
    mine = place // half
    swap = [(i, (i + half) % seq_size) for i in range(seq_size)]
    groups = [list(range(half)), list(range(half, seq_size))]
    by_chip = seq_size == 4 and utt_size == 8 and model == 768 and w_in.shape[2] == 3072

    def to_whole(array):
        far = lax.ppermute(pick(array, 1 - mine), "seq", swap)
        return jnp.concatenate([pick(array, mine), far], 0)

    def to_split(array):
        near, far = array[:block_rows], lax.ppermute(array[block_rows:], "seq", swap)
        first = jnp.where(mine == 0, near, far)
        second = jnp.where(mine == 0, far, near)
        return jnp.stack([first, second])

    def turn(array):
        return exchange(array, "seq", 1, seq_size) if by_chip else None

    if by_chip:
        members = [place, place ^ 1]
    else:
        members = [mine * half + i for i in range(half)]
    live_bits = pick(drop_bits, mine)
    values = [pick(lengths, mine), live_bits[0], live_bits[1], place % 2, place // 2]
    values += [utt_place % 2, utt_place // 2 % 2, utt_place // 4]
    for member in members:
        values += [member * block_rows, (member + half) % seq_size * block_rows]
    meta = jnp.stack(values)

    x = low = to_whole(frames)
    saved_all = []
    grad = None
    for layer in range(LAYERS):
        kv = project(meta, low, w_qkv, layer, attn_bias, model, 2 * model)
        if by_chip:
            key_values = [kv, turn(kv)]
        else:
            key_values = [lax.all_gather(kv, "seq", axis=0, tiled=True, axis_index_groups=groups)]
        q = project(meta, low, w_qkv, layer, attn_bias, 0, model, (kv,))
        att, extra = attend(meta, q, key_values, block_rows)
        nxt, next_low, *saved = feed(meta, x, att, layer, w_out, layer_bias, gains, w_in, in_bias, w_back)
        fars = (turn(low), turn(att), turn(saved[2]), turn(saved[3]))
        saved_all.append((low, q, key_values, att, extra, saved, fars))
        x, low = nxt, next_low
    mixed = to_split(low)

    grad = to_whole(cotangent)
    outputs = [None] * LAYERS
    if not by_chip:
        smalls = [None] * LAYERS
        for layer in reversed(range(LAYERS)):
            low, q, key_values, att, extra, saved, _ = saved_all[layer]
            sum_one, grad_att, pre, _, second, branch, _, small, grad_ibias = feed_back(
                meta, grad, saved, layer, w_out, gains, w_in, w_back
            )
            gq, bias_sums, gkv = attend_back(meta, q, grad_att, att, extra, key_values, block_rows)
            smalls[layer] = jnp.concatenate([small[:6], bias_sums[:2], grad_ibias.reshape(4, model)], 0)
            kind = f32 if layer > 0 else bf16
            gkv = lax.psum_scatter(gkv, "seq", scatter_dimension=1, tiled=True, axis_index_groups=groups)
            grad = project_back(meta, gq, gkv, jnp.zeros_like(gkv), grad, sum_one, w_qkv, layer, kind)
            products = [
                dot_tn(low, jnp.concatenate([gq, gkv[0], gkv[1]], 1)),
                dot_tn(att, branch),
                dot_tn(saved[2], pre),
                dot_tn(saved[3], second),
            ]
            shares = [
                lax.psum_scatter(product.astype(bf16), "utt", scatter_dimension=0, tiled=True)
                for product in products
            ]
            outputs[layer] = [lax.psum(share, "seq").astype(f32) for share in shares]
        grad_frames = to_split(grad)
        small = lax.psum(jnp.stack(smalls), ("utt", "seq"))
        unit = model // utt_size
        mine_small = lax.dynamic_slice_in_dim(small[:, :8], utt_place * unit, unit, 2)
        grad_ibias = small[:, 8:].reshape(LAYERS, 4 * model)
        grad_ibias = lax.dynamic_slice_in_dim(grad_ibias, 4 * utt_place * unit, 4 * unit, 1)
        grad_lbias, grad_gains, grad_abias = mine_small[:, 0:4], mine_small[:, 4:6], mine_small[:, 6:8]
        grad_wqkv, grad_wout, grad_win, grad_wback = (
            jnp.stack([per[member] for per in outputs]) for member in range(4)
        )
    else:
        low, q, key_values, att, extra, saved, fars = saved_all[1]
        sum_one, grad_att, pre, pre_send, second, branch, send, small, grad_ibias = feed_back(
            meta, grad, saved, 1, w_out, gains, w_in, w_back
        )
        small_part = (small, grad_ibias)
        pre_far, send_far = turn(pre_send), turn(send)
        gq, bias_sums, gkv, gkv_send, half_send = attend_back(
            meta, q, grad_att, att, extra, key_values, block_rows
        )
        smalls = [small, bias_sums, grad_ibias]
        gkv_far, half_far = turn(gkv_send), turn(half_send)
        feed_part = (saved[2], fars[2], pre, pre_far, att, fars[1], branch, saved[3], fars[3], second, send_far)
        group = weight_grads(meta, feed_part, None, None, (gq,))
        first = chain_steps(meta, group)
        ties = next(first)
        waiting = (low, fars[0], gq, gkv, gkv_far, gkv_send, half_far)
        grad = project_back(meta, gq, gkv, gkv_far, grad, sum_one, w_qkv, 1, f32, ties)

        low, q, key_values, att, extra, saved, fars = saved_all[0]
        sum_one, grad_att, pre, pre_send, second, branch, send, small, grad_ibias = feed_back(
            meta, grad, saved, 0, w_out, gains, w_in, w_back
        )
        pre_far, send_far = turn(pre_send), turn(send)
        ties = first.send((grad_att,))
        feed_part = (saved[2], fars[2], pre, pre_far, att, fars[1], branch, saved[3], fars[3], second, send_far)
        group = weight_grads(meta, feed_part, waiting, None, ties)
        second_chain = chain_steps(meta, group)
        ties = next(second_chain)
        gq, bias_sums, gkv, gkv_send, half_send = attend_back(
            meta, q, grad_att, att, extra, key_values, block_rows, ties
        )
        gkv_far, half_far = turn(gkv_send), turn(half_send)
        ties = first.send((gq,))
        ties = second_chain.send(ties)
        smalls = [small, bias_sums, grad_ibias] + smalls
        waiting = (low, fars[0], gq, gkv, gkv_far, gkv_send, half_far)
        group = weight_grads(meta, None, waiting, smalls, ties)
        third = chain_steps(meta, group)
        ties = next(third)
        grad = project_back(meta, gq, gkv, gkv_far, grad, sum_one, w_qkv, 0, bf16, ties)
        grad_frames = to_split(grad)
        ties = (grad,)
        done = {}
        chains = {"first": first, "second": second_chain, "third": third}
        while len(done) < 3:
            for name, steps in chains.items():
                if name not in done:
                    result = steps.send(ties)
                    if len(result) == 2:
                        ties, done[name] = result
                    else:
                        ties = result
        grad_win, grad_wout, grad_wback = finish(
            finish_feed_kernel,
            meta,
            done["second"] + done["first"],
            ((LAYERS, 96, 3072), (LAYERS, 96, 768), (LAYERS, 384, 768)),
            "finish_feed",
        )
        grad_wqkv, grad_abias, grad_lbias, grad_gains, grad_ibias = finish(
            finish_project_kernel,
            meta,
            done["third"] + done["second"],
            ((LAYERS, 96, 2304), (LAYERS, 2, 96), (LAYERS, 4, 96), (LAYERS, 2, 96), (LAYERS, 4, 96)),
            "finish_project",
        )
        grad_ibias = grad_ibias.reshape(LAYERS, 384)
    return (
        mixed,
        grad_frames,
        grad_wqkv,
        grad_abias,
        grad_wout,
        grad_lbias,
        grad_gains,
        grad_win,
        grad_ibias,
        grad_wback,
    )


def solution(mesh):
    frame_spec = P("utt", "seq", None)
    sizes = (mesh.shape["seq"], mesh.shape["utt"])
    return jax.shard_map(
        functools.partial(body, sizes),
        mesh=mesh,
        in_specs=(frame_spec, P("utt"), P("utt", None)) + (P(),) * 8 + (frame_spec,),
        out_specs=(
            frame_spec,
            frame_spec,
            P(None, "utt", None),
            P(None, None, "utt"),
            P(None, "utt", None),
            P(None, None, "utt"),
            P(None, None, "utt"),
            P(None, "utt", None),
            P(None, "utt"),
            P(None, "utt", None),
        ),
        check_vma=False,
    )
```
